32 devices in a mesh: dp: 4 (over x, core), adapter: 8 (over z, y).
Axes of the slice: x: 2, y: 2, z: 4, core: 2. Of those that a mesh axis runs over, the one named last changes fastest.
Arguments:
- residual_input: bfloat16 [16384, 2560], P(('dp', 'adapter')), may hold values from -6 to 6
- input_norm_gain: float32 [2560], replicated, may hold values from 0.5 to 1.5
- base_projection_weight: bfloat16 [2560, 4096], P('adapter', 'dp'), may hold values from -0.125 to 0.125
- query_key_gains: float32 [2, 256], replicated, may hold values from 0.5 to 1.5
- adapter_down_weight: bfloat16 [32, 2560, 48], P('adapter'), may hold values from -0.125 to 0.125
- adapter_up_weight: bfloat16 [32, 16, 4096], P('adapter'), may hold values from -1.5 to 1.5
- row_adapter_index: int32 [16384, 1], P(('dp', 'adapter')), may hold values from 0 to 31; in each aligned block of 512 rows (0 to 511, 512 to 1023, ...) at most 32 rows name the same one
- row_sequence_index: int32 [16384], P(('dp', 'adapter')), may hold values from 0 to 1, never falling along the last dimension, each value on 1 to 12288 neighbouring positions
Outputs:
- attended: bfloat16 [16384, 2048], P(('dp', 'adapter'))
The draws below stay inside these ranges and needn't reach their ends.
Inputs may be any that keep to these rules, and one draw needn't show every extreme that they name: `row_adapter_index`: among the rows of one device, no adapter serves more than 32 rows; some adapter serves exactly 32 rows of some device. `row_sequence_index`: sequence numbers never fall along the rows; every sequence has 1 to 12288 rows, one exactly 12288.
All inputs are finite; a program needn't handle non-finite values.
Results may differ from the reference program's by a relative error of at most 0.02.
Values may be sent and summed in bfloat16 or wider, within the bound.
No kernel may reach another device: no remote copies, remote signals or barrier semaphores. Data moves between devices by JAX's collectives and lax.ppermute only.
A program may use at most 128 MiB of HBM per device.

```python
import math
import jax
import jax.numpy as jnp
import numpy as np
from jax import lax

MODEL_WIDTH = 2560
HEADS = 8
KV_HEADS = 4
HEAD_DIM = 256
WINDOW = 1024
ADAPTER_RANK = 16
TOK_DEV = 512
PROJECTED_WIDTH = 4096
ADAPTER_TOTAL = 32
PACKED_ROWS = 16384
CAP = 32
SEG_COUNT = 2
SEG_MAX = 12288


def shard_levels(rng, shape, shards, smallest, largest):
    def one(position, shards_of):
        steps = jax.random.uniform(jax.random.fold_in(jax.random.fold_in(rng, 6), position), (shards_of,), jnp.float32, smallest / len(shards), largest / len(shards))
        return jnp.repeat(jnp.exp(steps), shape[position] // shards_of).reshape((-1,) + (1,) * (len(shape) - position - 1))

    factor_of = one(*shards[0])
    for cut in shards[1:]:
        factor_of = factor_of * one(*cut)
    return factor_of


def profile(count, total, reach, skew):
    loads = [(1 << 20) // math.isqrt(grade ** skew) + 1 for grade in range(2, count + 1)]
    spare, counts = total - reach - (count - 1), [1] * (count - 1)
    while spare > 0:
        candidates = [i for i in range(count - 1) if counts[i] < reach]
        whole, budget = sum([loads[i] for i in candidates]), spare
        for i in candidates:
            more = min(reach - counts[i], max(1, budget * loads[i] // whole), spare)
            counts[i] = counts[i] + more
            spare = spare - more
    return np.array([reach] + counts)


def ragged(stream_key, number_of, total, reach, slope):
    if number_of == 2:
        one = jax.random.randint(stream_key, (), max(1, total - reach), min(reach, total - 1) + 1)
        return jnp.stack([one, total - one])
    tallies = jnp.asarray(profile(number_of, total, reach, slope), jnp.int32)
    couples = (number_of - 1) // 2
    source_of, sink = tallies[1:1 + 2 * couples:2], tallies[2:2 + 2 * couples:2]
    margin = jnp.minimum(source_of - 1, reach - sink)
    passed = jax.random.randint(jax.random.fold_in(stream_key, 1), (couples,), 0, 1 << 20) % (margin + 1)
    tallies = tallies.at[1:1 + 2 * couples:2].set(source_of - passed).at[2:2 + 2 * couples:2].set(sink + passed)
    return tallies[jax.random.permutation(jax.random.fold_in(stream_key, 2), number_of)]


def shared_out(rng, own, number, rows, number_of, top, bound, slope):
    ranking = jax.random.permutation(rng, number_of)
    crowded, ordinary = load_shares(number_of, rows * top, bound, slope, True), load_shares(number_of, rows * top, bound, slope, False)
    places = jnp.arange(number_of)

    def named(lengths, turn):
        used = int((lengths > 0).sum())
        fixed = max(1, used // 4)
        shifted = fixed + (places - fixed + turn * (used - fixed)) % max(1, number_of - fixed)
        return jnp.zeros((number_of,), jnp.int32).at[ranking[jnp.where(places < fixed, places, shifted)]].set(jnp.asarray(lengths, jnp.int32))

    lengths = jnp.where(number % 4 == 0, named(crowded, number // 4), named(ordinary, number - number // 4 - 1))
    mixed = jax.random.permutation(jax.random.fold_in(own, 3), number_of)
    giver, taker = mixed[0:number_of // 2 * 2:2], mixed[1:number_of // 2 * 2:2]
    room = jnp.minimum(lengths[giver] - 1, bound - lengths[taker]) // 2
    room = jnp.where((giver == ranking[0]) | (taker == ranking[0]) | (lengths[taker] == 0), 0, jnp.maximum(room, 0))
    shifted = jax.random.randint(jax.random.fold_in(own, 4), (number_of // 2,), 0, 1 << 20) % (room + 1)
    lengths = lengths.at[giver].add(-shifted).at[taker].add(shifted)
    labels = jnp.searchsorted(jnp.cumsum(lengths), jnp.arange(rows * top), side="right").astype(jnp.int32)
    grid = labels.reshape(top, rows).T
    grid = grid[jax.random.permutation(jax.random.fold_in(own, 1), rows)]
    turn = jax.random.randint(jax.random.fold_in(own, 2), (rows, 1), 0, top)
    return jnp.take_along_axis(grid, (jnp.arange(top)[None, :] + turn) % top, axis=1)


def load_shares(amount, total, most, skew, full):
    loads = [(1 << 20) // math.isqrt(rank ** skew) + 1 for rank in range(1, amount + 1)]
    largest = most if full else min(most, max(-(-total // amount), total * loads[0] // sum(loads)))
    least = 1 if total - largest >= amount - 1 else 0
    holding, spare = [largest] + [least] * (amount - 1), total - largest - least * (amount - 1)
    while spare > 0:
        free = [i for i in range(1, amount) if holding[i] < largest] or [i for i in range(1, amount) if holding[i] < most]
        whole, left = sum([loads[i] for i in free]), spare
        for i in free:
            extra = min(most - holding[i], max(1, left * loads[i] // whole), spare)
            holding[i] = holding[i] + extra
            spare = spare - extra
    return np.array(holding)


def gaussian(rng, shape, spread, limit, cuts=(), held_as=jnp.bfloat16):
    array = spread * jax.random.normal(rng, shape, jnp.float32)
    if cuts:
        array = array * shard_levels(rng, shape, cuts, -0.22, 0.18)
    return jnp.clip(array, -limit, limit).astype(held_as)


def setup_inputs(seed: int = 0) -> dict:
    streams_of = jax.random.split(jax.random.key(seed), 9)
    residual_input = gaussian(streams_of[0], (PACKED_ROWS, MODEL_WIDTH), 1.0, 6.0, ((0, 32),))
    input_norm_gain = jnp.clip(1.0 + 0.1 * jax.random.normal(streams_of[1], (MODEL_WIDTH,), jnp.float32), 0.5, 1.5)
    base_projection_weight = gaussian(streams_of[2], (MODEL_WIDTH, PROJECTED_WIDTH), MODEL_WIDTH ** -0.5, 0.125, ((0, 8), (1, 4)))
    query_key_gains = jnp.clip(1.0 + 0.1 * jax.random.normal(streams_of[3], (2, HEAD_DIM), jnp.float32), 0.5, 1.5)
    adapter_down_weight = gaussian(streams_of[4], (ADAPTER_TOTAL, MODEL_WIDTH, 3 * ADAPTER_RANK), MODEL_WIDTH ** -0.5, 0.125, ((0, 8),))
    adapter_up_weight = gaussian(streams_of[5], (ADAPTER_TOTAL, ADAPTER_RANK, PROJECTED_WIDTH), ADAPTER_RANK ** -0.5, 1.5, ((0, 8),))
    row_adapter_index_keys = jax.random.split(jax.random.fold_in(streams_of[6], 1), PACKED_ROWS // TOK_DEV)
    row_adapter_index_turns = jax.random.permutation(jax.random.fold_in(streams_of[6], 3), PACKED_ROWS // TOK_DEV)
    row_adapter_index = jax.vmap(lambda own, number: shared_out(jax.random.fold_in(streams_of[6], 2), own, number, TOK_DEV, ADAPTER_TOTAL, 1, CAP, 2))(row_adapter_index_keys, row_adapter_index_turns).reshape((PACKED_ROWS, 1))
    row_sequence_index = jnp.searchsorted(jnp.cumsum(ragged(streams_of[7], SEG_COUNT, PACKED_ROWS, SEG_MAX, 2)), jnp.arange(PACKED_ROWS), side="right").astype(jnp.int32)
    return {"residual_input": residual_input, "input_norm_gain": input_norm_gain, "base_projection_weight": base_projection_weight, "query_key_gains": query_key_gains, "adapter_down_weight": adapter_down_weight, "adapter_up_weight": adapter_up_weight, "row_adapter_index": row_adapter_index, "row_sequence_index": row_sequence_index}


def head_norm(block, heads, gain):
    shaped = block.reshape(block.shape[0], heads, HEAD_DIM)
    scaled = shaped * lax.rsqrt(lax.optimization_barrier(jnp.mean(shaped * shaped, axis=-1, keepdims=True)) + 1e-06) * gain
    return scaled.astype(jnp.bfloat16)

def reference(residual_input, input_norm_gain, base_projection_weight, query_key_gains, adapter_down_weight, adapter_up_weight, row_adapter_index, row_sequence_index):
    width_q = HEADS * HEAD_DIM
    width_k = KV_HEADS * HEAD_DIM
    group = HEADS // KV_HEADS
    before = (WINDOW + TOK_DEV - 2) // TOK_DEV
    span = (before + 1) * TOK_DEV
    block_list = PACKED_ROWS // TOK_DEV
    values_in = residual_input.astype(jnp.float32)
    normed = (values_in * lax.rsqrt(lax.optimization_barrier(jnp.mean(values_in * values_in, axis=-1, keepdims=True)) + 1e-06) * input_norm_gain).astype(jnp.bfloat16)
    base = jnp.dot(normed, base_projection_weight, preferred_element_type=jnp.float32).astype(jnp.bfloat16)
    adapter_ids = row_adapter_index[:, 0].astype(jnp.int32)

    def adapter_block(adapter_index):
        start = (adapter_index * TOK_DEV).astype(jnp.int32)
        rows = lax.dynamic_slice_in_dim(normed, start, TOK_DEV, 0).astype(jnp.float32)
        chosen_adapter = lax.dynamic_slice_in_dim(adapter_ids, start, TOK_DEV, 0)
        down_projected_rows = jnp.take(adapter_down_weight, chosen_adapter, axis=0).astype(jnp.float32)
        rank_values = jnp.einsum('td,tdr->tr', rows, down_projected_rows).astype(jnp.bfloat16)
        rank_values = lax.optimization_barrier(rank_values).astype(jnp.float32)
        up_projected_rows = jnp.take(adapter_up_weight, chosen_adapter, axis=0).astype(jnp.float32)
        part_q = jnp.einsum('tr,trq->tq', rank_values[:, 0:ADAPTER_RANK], up_projected_rows[:, :, 0:width_q])
        part_k = jnp.einsum('tr,trq->tq', rank_values[:, ADAPTER_RANK:2 * ADAPTER_RANK], up_projected_rows[:, :, width_q:width_q + width_k])
        part_v = jnp.einsum('tr,trq->tq', rank_values[:, 2 * ADAPTER_RANK:3 * ADAPTER_RANK], up_projected_rows[:, :, width_q + width_k:])
        return jnp.concatenate([part_q, part_k, part_v], axis=1).astype(jnp.bfloat16)
    delta_update = lax.map(adapter_block, jnp.arange(block_list, dtype=jnp.int32)).reshape(PACKED_ROWS, PROJECTED_WIDTH)
    projected = base.astype(jnp.float32) + delta_update.astype(jnp.float32)
    queries = head_norm(projected[:, 0:width_q], HEADS, query_key_gains[0])
    keys = head_norm(projected[:, width_q:width_q + width_k], KV_HEADS, query_key_gains[1])
    values = projected[:, width_q + width_k:].astype(jnp.bfloat16).reshape(PACKED_ROWS, KV_HEADS, HEAD_DIM)
    pad = before * TOK_DEV
    keys_pad = jnp.concatenate([jnp.zeros((pad, KV_HEADS, HEAD_DIM), jnp.bfloat16), keys], axis=0)
    values_pad = jnp.concatenate([jnp.zeros((pad, KV_HEADS, HEAD_DIM), jnp.bfloat16), values], axis=0)
    seg_pad = jnp.concatenate([jnp.full((pad,), -1, jnp.int32), row_sequence_index.astype(jnp.int32)], axis=0)

    def attend_block(adapter_index):
        start = (adapter_index * TOK_DEV).astype(jnp.int32)
        query_block = lax.dynamic_slice_in_dim(queries, start, TOK_DEV, 0).reshape(TOK_DEV, KV_HEADS, group, HEAD_DIM)
        query_seg = lax.dynamic_slice_in_dim(row_sequence_index.astype(jnp.int32), start, TOK_DEV, 0)
        key_block = lax.dynamic_slice_in_dim(keys_pad, start, span, 0)
        value_block = lax.dynamic_slice_in_dim(values_pad, start, span, 0)
        key_seg = lax.dynamic_slice_in_dim(seg_pad, start, span, 0)
        query_pos = start + jnp.arange(TOK_DEV, dtype=jnp.int32)
        key_pos = start - pad + jnp.arange(span, dtype=jnp.int32)
        gap = query_pos[:, None] - key_pos[None, :]
        allowed = (query_seg[:, None] == key_seg[None, :]) & (gap >= 0) & (gap < WINDOW) & (key_pos[None, :] >= 0)
        scores = jnp.einsum('tkgd,skd->kgts', query_block.astype(jnp.float32), key_block.astype(jnp.float32)) * HEAD_DIM ** (-0.5)
        weights = jnp.where(allowed[None, None], jnp.exp(scores), jnp.float32(0.0))
        total = lax.optimization_barrier(jnp.sum(weights, axis=-1))
        probs = weights.astype(jnp.bfloat16)
        summed = jnp.einsum('kgts,skd->tkgd', probs.astype(jnp.float32), value_block.astype(jnp.float32))
        result = summed / jnp.transpose(total, (2, 0, 1))[..., None]
        return result.reshape(TOK_DEV, width_q).astype(jnp.bfloat16)
    return lax.map(attend_block, jnp.arange(block_list, dtype=jnp.int32)).reshape(PACKED_ROWS, width_q)
```

```python
import functools
import math

import jax
import jax.numpy as jnp
from jax import lax
from jax.experimental import pallas as pl
from jax.experimental.pallas import tpu as pltpu
from jax.sharding import PartitionSpec as P

HEADS = 8
KV_HEADS = 4
HEAD_DIM = 256
WINDOW = 1024


def shifted(value, axis, by):
    size = lax.axis_size(axis)
    pairs = [(i, i + by) for i in range(size) if 0 <= i + by < size]
    return lax.ppermute(value, axis, pairs)


def head_norm(block, heads, gain):
    shaped = block.reshape(block.shape[0], heads, HEAD_DIM)
    scaled = shaped * lax.rsqrt(jnp.mean(shaped * shaped, axis=-1, keepdims=True) + 1e-06) * gain
    return scaled.astype(jnp.bfloat16)


def adapter_delta(rank_values, up_matrices):
    width_q = HEADS * HEAD_DIM
    width_k = KV_HEADS * HEAD_DIM
    inner = up_matrices.shape[1]
    part_q = jnp.einsum(
        "nacr,arq->nacq",
        rank_values[..., 0:inner],
        up_matrices[:, :, 0:width_q],
        preferred_element_type=jnp.float32,
    )
    part_k = jnp.einsum(
        "nacr,arq->nacq",
        rank_values[..., inner : 2 * inner],
        up_matrices[:, :, width_q : width_q + width_k],
        preferred_element_type=jnp.float32,
    )
    part_v = jnp.einsum(
        "nacr,arq->nacq",
        rank_values[..., 2 * inner : 3 * inner],
        up_matrices[:, :, width_q + width_k :],
        preferred_element_type=jnp.float32,
    )
    return jnp.concatenate([part_q, part_k, part_v], axis=-1).astype(jnp.bfloat16)


def adapter_ranks(adapter_slots, down_matrices):
    return jnp.einsum(
        "nacd,adr->nacr", adapter_slots, down_matrices, preferred_element_type=jnp.float32
    ).astype(jnp.bfloat16)


def general_body(
    residual_input,
    input_norm_gain,
    base_projection_weight,
    query_key_gains,
    adapter_down_weight,
    adapter_up_weight,
    row_adapter_index,
    row_sequence_index,
):
    rows = residual_input.shape[0]
    width = residual_input.shape[1]
    width_q = HEADS * HEAD_DIM
    width_k = KV_HEADS * HEAD_DIM
    group = HEADS // KV_HEADS
    values_in = residual_input.astype(jnp.float32)
    normed = (
        values_in
        * lax.rsqrt(jnp.mean(values_in * values_in, axis=-1, keepdims=True) + 1e-06)
        * input_norm_gain
    ).astype(jnp.bfloat16)
    slab = lax.all_gather(base_projection_weight, "dp", axis=1, tiled=True)
    base = jnp.dot(
        normed,
        lax.all_gather(slab, "adapter", axis=0, tiled=True),
        preferred_element_type=jnp.float32,
    ).astype(jnp.bfloat16)
    total_width = base.shape[1]
    owners = lax.axis_size("adapter")
    local_adapter_count = adapter_down_weight.shape[0]
    adapters_all = owners * local_adapter_count
    capacity = 2 * rows // adapters_all
    adapter_ids = row_adapter_index[:, 0]
    onehot = (adapter_ids[:, None] == jnp.arange(adapters_all, dtype=jnp.int32)[None, :]).astype(
        jnp.int32
    )
    earlier = jnp.cumsum(onehot, axis=0) - onehot
    place = jnp.sum(earlier * onehot, axis=1)
    slot = adapter_ids * capacity + place
    scratch_buffer = jnp.zeros((adapters_all * capacity, width), jnp.bfloat16).at[slot].set(normed)
    scratch_buffer = scratch_buffer.reshape(owners, local_adapter_count, capacity, width)
    adapter_corrections = adapter_delta(
        adapter_ranks(
            lax.all_to_all(scratch_buffer, "adapter", split_axis=0, concat_axis=0, tiled=True),
            adapter_down_weight,
        ),
        adapter_up_weight,
    )
    returned = lax.all_to_all(
        adapter_corrections, "adapter", split_axis=0, concat_axis=0, tiled=True
    )
    delta_slots = returned.reshape(adapters_all * capacity, total_width)
    delta_update = delta_slots[slot]
    projected = base.astype(jnp.float32) + delta_update.astype(jnp.float32)
    queries = head_norm(projected[:, 0:width_q], HEADS, query_key_gains[0]).reshape(
        rows, KV_HEADS, group, HEAD_DIM
    )
    keys = head_norm(
        projected[:, width_q : width_q + width_k], KV_HEADS, query_key_gains[1]
    ).reshape(rows, width_k)
    values = projected[:, width_q + width_k :].astype(jnp.bfloat16)
    before = (WINDOW + rows - 2) // rows
    key_parts = []
    value_parts = []
    seg_parts = []
    for offset in range(before, 0, -1):
        moved_keys, moved_values, moved_seg = shifted(
            (keys, values, row_sequence_index), ("dp", "adapter"), offset
        )
        key_parts.append(moved_keys)
        value_parts.append(moved_values)
        seg_parts.append(moved_seg)
    key_parts.append(keys)
    value_parts.append(values)
    seg_parts.append(row_sequence_index)
    span = (before + 1) * rows
    key_all = jnp.concatenate(key_parts, axis=0).reshape(span, KV_HEADS, HEAD_DIM)
    value_all = jnp.concatenate(value_parts, axis=0).reshape(span, KV_HEADS, HEAD_DIM)
    seg_all = jnp.concatenate(seg_parts, axis=0)
    position = lax.axis_index(("dp", "adapter"))
    query_pos = position * rows + jnp.arange(rows, dtype=jnp.int32)
    key_pos = (position - before) * rows + jnp.arange(span, dtype=jnp.int32)
    gap = query_pos[:, None] - key_pos[None, :]
    allowed = (
        (row_sequence_index[:, None] == seg_all[None, :])
        & (gap >= 0)
        & (gap < WINDOW)
        & (key_pos[None, :] >= 0)
    )
    scores = jnp.einsum(
        "tkgd,skd->kgts", queries, key_all, preferred_element_type=jnp.float32
    ) * HEAD_DIM ** (-0.5)
    weights = jnp.where(allowed[None, None], jnp.exp(scores), jnp.float32(0.0))
    total = jnp.sum(weights, axis=-1)
    probs = weights.astype(jnp.bfloat16)
    summed = jnp.einsum("kgts,skd->tkgd", probs, value_all, preferred_element_type=jnp.float32)
    result = summed / jnp.transpose(total, (2, 0, 1))[..., None]
    return result.reshape(rows, width_q).astype(jnp.bfloat16)


BF16 = jnp.bfloat16
F32 = jnp.float32
ANY = pl.BlockSpec(memory_space=pl.ANY)
SMEM = pl.BlockSpec(memory_space=pltpu.SMEM)
VMEM = pl.BlockSpec(memory_space=pltpu.VMEM)
Q_ROW, KV_KIND, KV_ROW, UP_EVEN, UP_ODD, DOWN_ID = range(6)


def params(mib):
    return pltpu.CompilerParams(vmem_limit_bytes=mib << 20)


def route(value, depth, rule):
    pairs = []
    for x in range(2):
        for core in range(2):
            for z in range(depth):
                for y in range(2):
                    to = rule(x, core, z, y)
                    if to is not None:
                        source = (2 * x + core) * 2 * depth + 2 * z + y
                        pairs.append((source, (2 * to[0] + to[1]) * 2 * depth + 2 * to[2] + to[3]))
    return lax.ppermute(value, ("dp", "adapter"), pairs)


def row_norm(values, gain):
    values = values.astype(F32)
    scale = lax.rsqrt(jnp.mean(values * values, axis=-1, keepdims=True) + 1e-06)
    return (values * scale * gain).astype(BF16)


def copies_done(copies):
    for copy in copies:
        copy.start()
    for copy in copies:
        copy.wait()


def rank_kernel(count, *refs):
    scalars, ids, normed = refs[:3]
    pieces = refs[3 : 3 + count]
    out, down, sems = refs[3 + count :]
    deep = pieces[0].shape[0]
    copies_done(
        [
            pltpu.make_async_copy(pieces[i], down.at[pl.ds(i * deep, deep)], sems.at[i])
            for i in range(count)
        ]
    )
    every = lax.dot_general(
        down[...], normed[...], (((1,), (1,)), ((), ())), preferred_element_type=F32
    )
    total = jnp.zeros(out.shape, F32)
    for i in range(count):
        mine = ids[...] == scalars[DOWN_ID, i]
        total = total + jnp.where(mine, every[i * deep : (i + 1) * deep], 0.0)
    out[...] = total.astype(BF16)


def adapter_ranks_of(scalars, ids, normed, pieces):
    rows, width = normed.shape
    count, deep = len(pieces), pieces[0].shape[0]
    return pl.pallas_call(
        functools.partial(rank_kernel, count),
        out_shape=jax.ShapeDtypeStruct((deep, rows), BF16),
        in_specs=[SMEM, VMEM, VMEM] + [ANY] * count,
        out_specs=VMEM,
        scratch_shapes=[
            pltpu.VMEM((count * deep, width), BF16),
            pltpu.SemaphoreType.DMA((count,)),
        ],
        compiler_params=params(24),
        cost_estimate=pl.CostEstimate(
            flops=2 * rows * width * count * deep,
            bytes_accessed=2 * (rows + count * deep) * width,
            transcendentals=0,
        ),
    )(scalars, ids, normed, *pieces)


def spread(ranks, ids, scalars, count, into):
    inner = ranks.shape[0]
    for i in range(count):
        for odd in range(2):
            mine = ids[...] == scalars[UP_EVEN + odd, i]
            at = (2 * i + odd) * inner
            into[at : at + inner, :] = jnp.where(mine, ranks, jnp.zeros_like(ranks))


def project(normed, weight, into, up):
    base = jnp.dot(normed, weight, preferred_element_type=F32).astype(BF16)
    delta = lax.dot_general(
        into, up, (((0,), (0,)), ((), ())), preferred_element_type=F32
    ).astype(BF16)
    return base.astype(F32) + delta.astype(F32)


def unit(block, gain):
    scale = lax.rsqrt(jnp.mean(block * block, axis=-1, keepdims=True) + 1e-06)
    return (block * scale * gain).astype(BF16)


def kv_kernel(count, inner, *refs):
    scalars, ids, gains, normed, ranks_a, ranks_b = refs[:6]
    pieces = refs[6 : 6 + count]
    out, weight, up, into_k, into_v, sems = refs[6 + count :]
    deep = pieces[0].shape[0] - 4 * inner
    copies = []
    for i in range(count):
        kind = scalars[KV_KIND, i]
        row = pl.multiple_of(scalars[KV_ROW, i], deep)
        copies.append(
            pltpu.make_async_copy(
                pieces[i].at[pl.ds(0, deep)], weight.at[kind, pl.ds(row, deep)], sems.at[3 * i]
            )
        )
        for both in range(2):
            copies.append(
                pltpu.make_async_copy(
                    pieces[i].at[pl.ds(deep + 2 * inner * both, 2 * inner)],
                    up.at[both, pl.ds(2 * inner * i, 2 * inner)],
                    sems.at[3 * i + 1 + both],
                )
            )
    for copy in copies:
        copy.start()
    ranks = ranks_a[...] + ranks_b[...]
    spread(ranks[inner : 2 * inner], ids, scalars, count, into_k)
    spread(ranks[2 * inner : 3 * inner], ids, scalars, count, into_v)
    for copy in copies:
        copy.wait()
    for head in range(weight.shape[2] // HEAD_DIM):
        cut = slice(head * HEAD_DIM, (head + 1) * HEAD_DIM)
        keys = project(normed[...], weight[0, :, cut], into_k[...], up[0, :, cut])
        out[head, :, 0:HEAD_DIM] = unit(keys, gains[1:2, :])
        values = project(normed[...], weight[1, :, cut], into_v[...], up[1, :, cut])
        out[head, :, HEAD_DIM:] = values.astype(BF16)


def keys_values(scalars, ids, gains, normed, ranks_a, ranks_b, pieces):
    rows, width = normed.shape
    count, inner = len(pieces), ranks_a.shape[0] // 3
    columns = pieces[0].shape[1]
    heads = columns // HEAD_DIM
    return pl.pallas_call(
        functools.partial(kv_kernel, count, inner),
        out_shape=jax.ShapeDtypeStruct((heads, rows, 2 * HEAD_DIM), BF16),
        in_specs=[SMEM, VMEM, VMEM, VMEM, VMEM, VMEM] + [ANY] * count,
        out_specs=VMEM,
        scratch_shapes=[
            pltpu.VMEM((2, width, columns), BF16),
            pltpu.VMEM((2, 2 * inner * count, columns), BF16),
            pltpu.VMEM((2 * inner * count, rows), BF16),
            pltpu.VMEM((2 * inner * count, rows), BF16),
            pltpu.SemaphoreType.DMA((3 * count,)),
        ],
        compiler_params=params(32),
        cost_estimate=pl.CostEstimate(
            flops=4 * rows * width * columns,
            bytes_accessed=2 * (rows + 2 * columns) * width,
            transcendentals=0,
        ),
    )(scalars, ids, gains, normed, ranks_a, ranks_b, *pieces)


def query_kernel(count, inner, *refs):
    scalars, ids_own, ids_nb, gains, normed_own, normed_nb = refs[:6]
    ranks = refs[6:10]
    pieces = refs[10 : 10 + count]
    out_own, out_nb, weight, up, into_own, into_nb, sems = refs[10 + count :]
    deep = pieces[0].shape[0] - 2 * inner
    copies = []
    for i in range(count):
        row = pl.multiple_of(scalars[Q_ROW, i], deep)
        copies.append(
            pltpu.make_async_copy(
                pieces[i].at[pl.ds(0, deep)], weight.at[pl.ds(row, deep)], sems.at[2 * i]
            )
        )
        copies.append(
            pltpu.make_async_copy(
                pieces[i].at[pl.ds(deep, 2 * inner)],
                up.at[pl.ds(2 * inner * i, 2 * inner)],
                sems.at[2 * i + 1],
            )
        )
    for copy in copies:
        copy.start()
    spread(ranks[0][0:inner] + ranks[1][0:inner], ids_own, scalars, count, into_own)
    spread(ranks[2][0:inner] + ranks[3][0:inner], ids_nb, scalars, count, into_nb)
    for copy in copies:
        copy.wait()
    for head in range(weight.shape[1] // HEAD_DIM):
        cut = slice(head * HEAD_DIM, (head + 1) * HEAD_DIM)
        for normed, into, out in ((normed_nb, into_nb, out_nb), (normed_own, into_own, out_own)):
            block = project(normed[...], weight[:, cut], into[...], up[:, cut])
            out[:, cut] = unit(block, gains[0:1, :])


def queries_of(scalars, ids_own, ids_nb, gains, normed_own, normed_nb, ranks, pieces):
    rows, width = normed_own.shape
    count, inner = len(pieces), ranks[0].shape[0] // 3
    columns = pieces[0].shape[1]
    return pl.pallas_call(
        functools.partial(query_kernel, count, inner),
        out_shape=[jax.ShapeDtypeStruct((rows, columns), BF16)] * 2,
        in_specs=[SMEM] + [VMEM] * 9 + [ANY] * count,
        out_specs=[VMEM, VMEM],
        scratch_shapes=[
            pltpu.VMEM((width, columns), BF16),
            pltpu.VMEM((2 * inner * count, columns), BF16),
            pltpu.VMEM((2 * inner * count, rows), BF16),
            pltpu.VMEM((2 * inner * count, rows), BF16),
            pltpu.SemaphoreType.DMA((2 * count,)),
        ],
        compiler_params=params(40),
        cost_estimate=pl.CostEstimate(
            flops=4 * rows * width * columns,
            bytes_accessed=2 * (2 * rows + columns) * width,
            transcendentals=0,
        ),
    )(scalars, ids_own, ids_nb, gains, normed_own, normed_nb, *ranks, *pieces)


def attend_kernel(places, queries, seg_rows, seg_keys, *refs):
    blocks, out, held, sems = refs[:4], refs[4], refs[5], refs[6]
    rows = queries.shape[0]
    slots = held.shape[0]
    for wait in (False, True):
        for i in range(4):
            slot = places[i]

            @pl.when((slot >= 0) & (slot < slots))
            def _():
                copy = pltpu.make_async_copy(blocks[i], held.at[slot], sems.at[i])
                if wait:
                    copy.wait()
                else:
                    copy.start()

    tile = HEAD_DIM
    heads = queries.shape[1] // HEAD_DIM
    tiles = WINDOW // tile + 1
    per_block = rows // tile
    row = lax.broadcasted_iota(jnp.int32, (tile, tile), 0)
    column = lax.broadcasted_iota(jnp.int32, (tile, tile), 1)
    for part in range(rows // tile):
        here = slice(part * tile, (part + 1) * tile)
        query = jnp.concatenate(
            [queries[here, h * HEAD_DIM : (h + 1) * HEAD_DIM] for h in range(heads)], axis=0
        )
        total = jnp.zeros((heads * tile, 128), F32)
        summed = jnp.zeros((heads * tile, HEAD_DIM), F32)
        for step in range(tiles):
            at = part + step
            block, inside = at // per_block, at % per_block
            span = slice(inside * tile, (inside + 1) * tile)
            keys = held[block, span, 0:HEAD_DIM]
            values = held[block, span, HEAD_DIM:]
            allowed = seg_rows[here, :] == seg_keys[:, at * tile : (at + 1) * tile]
            if step == 0:
                allowed = allowed & (column > row)
            if step == tiles - 1:
                allowed = allowed & (column <= row)
            scores = lax.dot_general(
                query, keys, (((1,), (1,)), ((), ())), preferred_element_type=F32
            )
            weights = jnp.exp2(scores * (HEAD_DIM ** (-0.5) * math.log2(math.e)))
            weights = jnp.where(jnp.concatenate([allowed] * heads, axis=0), weights, 0.0)
            for cut in range(tile // 128):
                total = total + weights[:, cut * 128 : (cut + 1) * 128]
            summed = summed + jnp.dot(
                weights.astype(BF16), values, preferred_element_type=F32
            )
        result = summed / jnp.sum(total, axis=-1, keepdims=True)
        for h in range(heads):
            out[here, h * HEAD_DIM : (h + 1) * HEAD_DIM] = result[
                h * tile : (h + 1) * tile
            ].astype(BF16)


def attend(head, places, queries, seg_rows, seg_keys, blocks):
    rows = queries.shape[0]
    width = queries.shape[1] // 2
    slots = seg_keys.shape[1] // rows
    return pl.pallas_call(
        attend_kernel,
        grid=(1,),
        out_shape=jax.ShapeDtypeStruct((rows, width), BF16),
        in_specs=[
            SMEM,
            pl.BlockSpec((rows, width), lambda i: (0, head)),
            pl.BlockSpec((rows, 1), lambda i: (0, 0)),
            pl.BlockSpec((1, slots * rows), lambda i: (0, 0)),
        ]
        + [ANY] * 4,
        out_specs=pl.BlockSpec((rows, width), lambda i: (0, 0)),
        scratch_shapes=[
            pltpu.VMEM((slots, rows, 2 * HEAD_DIM), BF16),
            pltpu.SemaphoreType.DMA((4,)),
        ],
        compiler_params=params(24),
        cost_estimate=pl.CostEstimate(
            flops=4 * rows * width * (WINDOW + HEAD_DIM),
            bytes_accessed=2 * rows * HEAD_DIM * 12,
            transcendentals=2 * rows * (WINDOW + HEAD_DIM),
        ),
    )(places, queries, seg_rows, seg_keys, *blocks)


def paired_body(
    residual_input,
    input_norm_gain,
    base_projection_weight,
    query_key_gains,
    adapter_down_weight,
    adapter_up_weight,
    row_adapter_index,
    row_sequence_index,
):
    rows = residual_input.shape[0]
    width_q, width_k = HEADS * HEAD_DIM, KV_HEADS * HEAD_DIM
    half_q, half_k = width_q // 2, width_k // 2
    depth = lax.axis_size("adapter") // 2
    local = adapter_down_weight.shape[0]
    deep = base_projection_weight.shape[0]
    place = lax.axis_index("dp")
    x, core = place // 2, place % 2
    owner = lax.axis_index("adapter")
    z, y = owner // 2, owner % 2
    swap_y = lambda v: route(v, depth, lambda x, c, z, y: (x, c, z, 1 - y))
    swap_x = lambda v: route(v, depth, lambda x, c, z, y: (1 - x, c, z, y))
    swap_core = lambda v: route(v, depth, lambda x, c, z, y: (x, 1 - c, z, y))
    ring = lambda v: route(v, depth, lambda x, c, z, y: (x, c, (z + 1) % depth, y))

    def onward(x, c, z, y):
        if z + 1 < depth:
            return (x, c, z + 1, y)
        after = 2 * x + c + 1
        return (after // 2, after % 2, 0, y) if after < 4 else None

    halo = lambda v: route(v, depth, onward)

    block = base_projection_weight
    top, bottom = block[: deep // 2], block[deep // 2 :]
    mine = lax.dynamic_slice_in_dim(block, y * half_k, half_k, 1)
    theirs = lax.dynamic_slice_in_dim(block, (1 - y) * half_k, half_k, 1)
    got_top = route(top, depth, lambda x, c, z, y: (0, y, z, c) if x == 0 and c != y else None)
    got_bottom = route(bottom, depth, lambda x, c, z, y: (1, y, z, c) if x == 0 else None)
    got_theirs = route(
        theirs,
        depth,
        lambda x, c, z, y: None if x == 0 else (1, c, z, 1) if y == 0 else (0, c, z, 0),
    )
    got_mine = route(mine, depth, lambda x, c, z, y: (0, c, z, 1) if x == 1 and y == 1 else None)
    share_q = jnp.where(x == 1, got_bottom, jnp.where(core == y, top, got_top))
    share_kv = jnp.where(
        x == 0, jnp.where(y == 0, got_theirs, got_mine), jnp.where(y == 0, mine, got_theirs)
    )
    up_one = lax.dynamic_index_in_dim(adapter_up_weight, place, 0, keepdims=False)

    def up_half(which):
        return (
            lax.dynamic_slice_in_dim(up_one, which * half_q, half_q, 1),
            lax.dynamic_slice_in_dim(up_one, width_q + which * half_k, half_k, 1),
            lax.dynamic_slice_in_dim(up_one, width_q + width_k + which * half_k, half_k, 1),
        )

    up_own = jnp.concatenate(up_half(y), axis=1)
    up_other = swap_y(jnp.concatenate(up_half(1 - y), axis=1))
    up_pair = jnp.concatenate(
        [jnp.where(y == 0, up_own, up_other), jnp.where(y == 0, up_other, up_own)], axis=0
    )
    share_q = jnp.concatenate([share_q, up_pair[:, :half_q]], axis=0)
    share_kv = jnp.concatenate(
        [share_kv, up_pair[:, half_q : half_q + half_k], up_pair[:, half_q + half_k :]], axis=0
    )
    share_down = lax.dynamic_index_in_dim(adapter_down_weight, place, 0, keepdims=False).T

    other_input = swap_y(residual_input)
    numbers = jnp.stack([row_adapter_index[:, 0], row_sequence_index])
    other_numbers = swap_y(numbers)
    ids_own, ids_nb = numbers[0:1], other_numbers[0:1]
    seg_pair = jnp.where(
        y == 0,
        jnp.concatenate([numbers[1], other_numbers[1]]),
        jnp.concatenate([other_numbers[1], numbers[1]]),
    )
    seg_before = jnp.where((place == 0) & (z == 0), -1, halo(seg_pair))
    seg_span = jnp.concatenate([seg_before, seg_pair])
    normed_own = row_norm(residual_input, input_norm_gain)
    normed_nb = row_norm(other_input, input_norm_gain)

    def gathered(share):
        pieces = []
        for step in range(depth):
            if step:
                share = ring(share)
            across = swap_x(share)
            pieces += [share, across, swap_core(share), swap_core(across)]
        return pieces

    down_pieces = gathered(share_down)
    kv_pieces = gathered(share_kv)
    q_pieces = gathered(share_q)
    table = []
    for step in range(depth):
        chunk = (z + depth - step) % depth
        for flip_x, flip_core in ((0, 0), (1, 0), (0, 1), (1, 1)):
            at_x = x + flip_x * (1 - 2 * x)
            at_core = core + flip_core * (1 - 2 * core)
            adapter = 2 * chunk * local + 2 * at_x + at_core
            table.append(
                jnp.stack(
                    [
                        (2 * chunk + at_core) * deep + at_x * (deep // 2),
                        at_core,
                        (2 * chunk + 1 - at_x) * deep,
                        adapter,
                        adapter + local,
                        adapter + y * local,
                    ]
                )
            )
    scalars = jnp.stack(table, axis=1).astype(jnp.int32)

    part_own = adapter_ranks_of(scalars, ids_own, normed_own, down_pieces)
    part_nb = adapter_ranks_of(scalars, ids_nb, normed_nb, down_pieces)
    back_nb = swap_y(part_own)
    back_own = swap_y(part_nb)
    gains = query_key_gains
    kv_own = keys_values(scalars, ids_own, gains, normed_own, part_own, back_own, kv_pieces)
    kv_nb = keys_values(scalars, ids_nb, gains, normed_nb, part_nb, back_nb, kv_pieces)
    queries_own, queries_nb = queries_of(
        scalars,
        ids_own,
        ids_nb,
        gains,
        normed_own,
        normed_nb,
        (part_own, back_own, part_nb, back_nb),
        q_pieces,
    )

    spans = {}
    for name, parity in (("own", y), ("nb", 1 - y)):
        seg_keys = lax.dynamic_slice_in_dim(seg_span, parity * rows, 3 * rows, 0)[None, :]
        seg_rows = lax.dynamic_slice_in_dim(seg_pair, parity * rows, rows, 0)[:, None]
        places = jnp.stack([y, 1 - y, 2 + y, 3 - y]) - parity
        spans[name] = (places.astype(jnp.int32), seg_rows, seg_keys)
    left, right = [], []
    for head in range(kv_own.shape[0]):
        blocks = (halo(kv_own[head]), halo(kv_nb[head]), kv_own[head], kv_nb[head])
        places, seg_rows, seg_keys = spans["nb"]
        sent = attend(head, places, queries_nb, seg_rows, seg_keys, blocks)
        places, seg_rows, seg_keys = spans["own"]
        kept = attend(head, places, queries_own, seg_rows, seg_keys, blocks)
        got = swap_y(sent)
        left.append(jnp.where(y == 0, kept, got))
        right.append(jnp.where(y == 0, got, kept))
    return jnp.concatenate(left + right, axis=1)


def paired(mesh, shapes):
    residual, _, weight, _, down = shapes[:5]
    rows = residual[0] // mesh.size
    return (
        mesh.shape["dp"] == 4
        and mesh.shape["adapter"] % 2 == 0
        and down[0] // mesh.shape["adapter"] == 4
        and rows % HEAD_DIM == 0
        and 2 * rows == WINDOW
        and weight[1] == (HEADS + 2 * KV_HEADS) * HEAD_DIM
        and weight[0] // mesh.shape["adapter"] % 32 == 0
    )


def solution(mesh):
    placed = (
        P(("dp", "adapter"), None),
        P(),
        P("adapter", "dp"),
        P(),
        P("adapter", None, None),
        P("adapter", None, None),
        P(("dp", "adapter"), None),
        P(("dp", "adapter")),
    )

    def whole(*arrays):
        body = paired_body if paired(mesh, [a.shape for a in arrays]) else general_body
        return jax.shard_map(
            body, mesh=mesh, in_specs=placed, out_specs=P(("dp", "adapter"), None), check_vma=False
        )(*arrays)

    return whole
```

```python
import functools
import math

import jax
import jax.numpy as jnp
import numpy as np
from jax import lax
from jax.experimental import pallas as pl
from jax.experimental.pallas import tpu as pltpu
from jax.sharding import PartitionSpec as P

HEADS = 8
KV_HEADS = 4
HEAD_DIM = 256
WINDOW = 1024


def shifted(value, axis, by):
    size = lax.axis_size(axis)
    pairs = [(i, i + by) for i in range(size) if 0 <= i + by < size]
    return lax.ppermute(value, axis, pairs)


def head_norm(block, heads, gain):
    shaped = block.reshape(block.shape[0], heads, HEAD_DIM)
    scaled = shaped * lax.rsqrt(jnp.mean(shaped * shaped, axis=-1, keepdims=True) + 1e-06) * gain
    return scaled.astype(jnp.bfloat16)


def adapter_delta(rank_values, up_matrices):
    width_q = HEADS * HEAD_DIM
    width_k = KV_HEADS * HEAD_DIM
    inner = up_matrices.shape[1]
    part_q = jnp.einsum(
        "nacr,arq->nacq",
        rank_values[..., 0:inner],
        up_matrices[:, :, 0:width_q],
        preferred_element_type=jnp.float32,
    )
    part_k = jnp.einsum(
        "nacr,arq->nacq",
        rank_values[..., inner : 2 * inner],
        up_matrices[:, :, width_q : width_q + width_k],
        preferred_element_type=jnp.float32,
    )
    part_v = jnp.einsum(
        "nacr,arq->nacq",
        rank_values[..., 2 * inner : 3 * inner],
        up_matrices[:, :, width_q + width_k :],
        preferred_element_type=jnp.float32,
    )
    return jnp.concatenate([part_q, part_k, part_v], axis=-1).astype(jnp.bfloat16)


def adapter_ranks(adapter_slots, down_matrices):
    return jnp.einsum(
        "nacd,adr->nacr", adapter_slots, down_matrices, preferred_element_type=jnp.float32
    ).astype(jnp.bfloat16)


def general_body(
    residual_input,
    input_norm_gain,
    base_projection_weight,
    query_key_gains,
    adapter_down_weight,
    adapter_up_weight,
    row_adapter_index,
    row_sequence_index,
):
    rows = residual_input.shape[0]
    width = residual_input.shape[1]
    width_q = HEADS * HEAD_DIM
    width_k = KV_HEADS * HEAD_DIM
    group = HEADS // KV_HEADS
    values_in = residual_input.astype(jnp.float32)
    normed = (
        values_in
        * lax.rsqrt(jnp.mean(values_in * values_in, axis=-1, keepdims=True) + 1e-06)
        * input_norm_gain
    ).astype(jnp.bfloat16)
    slab = lax.all_gather(base_projection_weight, "dp", axis=1, tiled=True)
    base = jnp.dot(
        normed,
        lax.all_gather(slab, "adapter", axis=0, tiled=True),
        preferred_element_type=jnp.float32,
    ).astype(jnp.bfloat16)
    total_width = base.shape[1]
    owners = lax.axis_size("adapter")
    local_adapter_count = adapter_down_weight.shape[0]
    adapters_all = owners * local_adapter_count
    capacity = 2 * rows // adapters_all
    adapter_ids = row_adapter_index[:, 0]
    onehot = (adapter_ids[:, None] == jnp.arange(adapters_all, dtype=jnp.int32)[None, :]).astype(
        jnp.int32
    )
    earlier = jnp.cumsum(onehot, axis=0) - onehot
    place = jnp.sum(earlier * onehot, axis=1)
    slot = adapter_ids * capacity + place
    scratch_buffer = jnp.zeros((adapters_all * capacity, width), jnp.bfloat16).at[slot].set(normed)
    scratch_buffer = scratch_buffer.reshape(owners, local_adapter_count, capacity, width)
    adapter_corrections = adapter_delta(
        adapter_ranks(
            lax.all_to_all(scratch_buffer, "adapter", split_axis=0, concat_axis=0, tiled=True),
            adapter_down_weight,
        ),
        adapter_up_weight,
    )
    returned = lax.all_to_all(
        adapter_corrections, "adapter", split_axis=0, concat_axis=0, tiled=True
    )
    delta_slots = returned.reshape(adapters_all * capacity, total_width)
    delta_update = delta_slots[slot]
    projected = base.astype(jnp.float32) + delta_update.astype(jnp.float32)
    queries = head_norm(projected[:, 0:width_q], HEADS, query_key_gains[0]).reshape(
        rows, KV_HEADS, group, HEAD_DIM
    )
    keys = head_norm(
        projected[:, width_q : width_q + width_k], KV_HEADS, query_key_gains[1]
    ).reshape(rows, width_k)
    values = projected[:, width_q + width_k :].astype(jnp.bfloat16)
    before = (WINDOW + rows - 2) // rows
    key_parts = []
    value_parts = []
    seg_parts = []
    for offset in range(before, 0, -1):
        moved_keys, moved_values, moved_seg = shifted(
            (keys, values, row_sequence_index), ("dp", "adapter"), offset
        )
        key_parts.append(moved_keys)
        value_parts.append(moved_values)
        seg_parts.append(moved_seg)
    key_parts.append(keys)
    value_parts.append(values)
    seg_parts.append(row_sequence_index)
    span = (before + 1) * rows
    key_all = jnp.concatenate(key_parts, axis=0).reshape(span, KV_HEADS, HEAD_DIM)
    value_all = jnp.concatenate(value_parts, axis=0).reshape(span, KV_HEADS, HEAD_DIM)
    seg_all = jnp.concatenate(seg_parts, axis=0)
    position = lax.axis_index(("dp", "adapter"))
    query_pos = position * rows + jnp.arange(rows, dtype=jnp.int32)
    key_pos = (position - before) * rows + jnp.arange(span, dtype=jnp.int32)
    gap = query_pos[:, None] - key_pos[None, :]
    allowed = (
        (row_sequence_index[:, None] == seg_all[None, :])
        & (gap >= 0)
        & (gap < WINDOW)
        & (key_pos[None, :] >= 0)
    )
    scores = jnp.einsum(
        "tkgd,skd->kgts", queries, key_all, preferred_element_type=jnp.float32
    ) * HEAD_DIM ** (-0.5)
    weights = jnp.where(allowed[None, None], jnp.exp(scores), jnp.float32(0.0))
    total = jnp.sum(weights, axis=-1)
    probs = weights.astype(jnp.bfloat16)
    summed = jnp.einsum("kgts,skd->tkgd", probs, value_all, preferred_element_type=jnp.float32)
    result = summed / jnp.transpose(total, (2, 0, 1))[..., None]
    return result.reshape(rows, width_q).astype(jnp.bfloat16)


BF16 = jnp.bfloat16
F32 = jnp.float32
ANY = pl.BlockSpec(memory_space=pl.ANY)
SMEM = pl.BlockSpec(memory_space=pltpu.SMEM)
VMEM = pl.BlockSpec(memory_space=pltpu.VMEM)
SMALL = pl.CostEstimate(flops=1, bytes_accessed=1, transcendentals=0)
Q_ROW, KV_KIND, KV_ROW, UP_EVEN, UP_ODD, DOWN_ID = range(6)


def params(mib):
    return pltpu.CompilerParams(vmem_limit_bytes=mib << 20)


def route(value, depth, rule):
    pairs = []
    for x in range(2):
        for core in range(2):
            for z in range(depth):
                for y in range(2):
                    to = rule(x, core, z, y)
                    if to is not None:
                        source = (2 * x + core) * 2 * depth + 2 * z + y
                        pairs.append((source, (2 * to[0] + to[1]) * 2 * depth + 2 * to[2] + to[3]))
    return lax.ppermute(value, ("dp", "adapter"), pairs)


def after(value, *others):
    return lax.optimization_barrier((value, others))[0]


def row_norm(values, gain):
    values = values.astype(F32)
    scale = lax.rsqrt(jnp.mean(values * values, axis=-1, keepdims=True) + 1e-06)
    return (values * scale * gain).astype(BF16)


def copies_done(copies):
    for copy in copies:
        copy.start()
    for copy in copies:
        copy.wait()


def masked_ranks(scalars, ids, down, normed, out, count):
    deep = out.shape[0]
    every = lax.dot_general(
        down[...], normed[...], (((1,), (1,)), ((), ())), preferred_element_type=F32
    )
    total = jnp.zeros(out.shape, F32)
    for i in range(count):
        mine = ids[...] == scalars[DOWN_ID, i]
        total = total + jnp.where(mine, every[i * deep : (i + 1) * deep], 0.0)
    out[...] = total.astype(BF16)


def rank_kernel(count, scalars, ids, normed, down, out):
    masked_ranks(scalars, ids, down, normed, out, count)


def first_rank_kernel(pieces, scalars, ids, normed, *refs):
    held = refs[: len(pieces.arrays)]
    out, down, sems = refs[len(pieces.arrays) :]
    deep, count = pieces.deep, len(pieces.names)
    copies = [
        pltpu.make_async_copy(
            pieces.cut(held, i, 0, deep), down.at[pl.ds(i * deep, deep)], sems.at[i]
        )
        for i in range(count)
    ]
    for copy in copies:
        copy.start()
    for copy in copies:
        copy.wait()
    masked_ranks(scalars, ids, down, normed, out, count)


def first_ranks(scalars, ids, normed, pieces):
    rows, width = normed.shape
    count, deep = len(pieces.names), pieces.deep
    return pl.pallas_call(
        functools.partial(first_rank_kernel, pieces),
        out_shape=[
            jax.ShapeDtypeStruct((deep, rows), BF16),
            jax.ShapeDtypeStruct((count * deep, width), BF16),
        ],
        in_specs=[SMEM, VMEM, VMEM] + [ANY] * len(pieces.arrays),
        out_specs=[VMEM, VMEM],
        scratch_shapes=[pltpu.SemaphoreType.DMA((count,))],
        compiler_params=params(24),
        cost_estimate=SMALL,
    )(scalars, ids, normed, *pieces.arrays)


def more_ranks(scalars, ids, normed, down, count):
    rows, width = normed.shape
    return pl.pallas_call(
        functools.partial(rank_kernel, count),
        out_shape=jax.ShapeDtypeStruct((down.shape[0] // count, rows), BF16),
        in_specs=[SMEM, VMEM, VMEM, VMEM],
        out_specs=VMEM,
        compiler_params=params(24),
        cost_estimate=SMALL,
    )(scalars, ids, normed, down)


def spread(ranks, ids, scalars, count, into):
    inner = ranks.shape[0]
    for i in range(count):
        for odd in range(2):
            mine = ids[...] == scalars[UP_EVEN + odd, i]
            at = (2 * i + odd) * inner
            into[at : at + inner, :] = jnp.where(mine, ranks, jnp.zeros_like(ranks))


def project(normed, weight, into, up):
    base = jnp.dot(normed, weight, preferred_element_type=F32).astype(BF16)
    delta = lax.dot_general(
        into, up, (((0,), (0,)), ((), ())), preferred_element_type=F32
    ).astype(BF16)
    return base.astype(F32) + delta.astype(F32)


def unit(block, gain):
    scale = lax.rsqrt(jnp.mean(block * block, axis=-1, keepdims=True) + 1e-06)
    return (block * scale * gain).astype(BF16)


class Pieces:
    def __init__(self, arrays, names, deep):
        self.arrays, self.names, self.deep = arrays, names, deep

    def cut(self, refs, i, start, size, columns=None):
        array, at = self.names[i]
        rows = pl.ds(at * self.deep + start, size)
        return refs[array].at[rows] if columns is None else refs[array].at[rows, columns]


def kv_kernel(pieces, inner, head, *refs):
    scalars, ids_own, ids_nb, gains = refs[:4]
    ranks = refs[4:8]
    normed = refs[8:10]
    held = refs[10 : 10 + len(pieces.arrays)]
    out, weight, up, into, sems = refs[10 + len(pieces.arrays) :]
    deep, count = pieces.deep - 4 * inner, len(pieces.names)
    columns = pl.ds(head * HEAD_DIM, HEAD_DIM)
    copies = []
    for i in range(count):
        kind = scalars[KV_KIND, i]
        row = pl.multiple_of(scalars[KV_ROW, i], deep)
        copies.append(
            pltpu.make_async_copy(
                pieces.cut(held, i, 0, deep, columns),
                weight.at[kind, pl.ds(row, deep)],
                sems.at[3 * i],
            )
        )
        for both in range(2):
            copies.append(
                pltpu.make_async_copy(
                    pieces.cut(held, i, deep + 2 * inner * both, 2 * inner, columns),
                    up.at[both, pl.ds(2 * inner * i, 2 * inner)],
                    sems.at[3 * i + 1 + both],
                )
            )
    for copy in copies:
        copy.start()
    for side, ids in ((0, ids_own), (1, ids_nb)):
        both = ranks[2 * side][...] + ranks[2 * side + 1][...]
        for kind in range(2):
            part = both[(1 + kind) * inner : (2 + kind) * inner]
            spread(part, ids, scalars, count, into.at[2 * side + kind])
    for copy in copies:
        copy.wait()
    for side in range(2):
        keys = project(normed[side][...], weight[0], into[2 * side], up[0])
        out[side, :, 0:HEAD_DIM] = unit(keys, gains[1:2, :])
        values = project(normed[side][...], weight[1], into[2 * side + 1], up[1])
        out[side, :, HEAD_DIM:] = values.astype(BF16)


def keys_values(head, scalars, ids_own, ids_nb, gains, ranks, normed_own, normed_nb, pieces):
    rows, width = normed_own.shape
    count, inner = len(pieces.names), ranks[0].shape[0] // 3
    return pl.pallas_call(
        functools.partial(kv_kernel, pieces, inner, head),
        out_shape=jax.ShapeDtypeStruct((2, rows, 2 * HEAD_DIM), BF16),
        in_specs=[SMEM] + [VMEM] * 9 + [ANY] * len(pieces.arrays),
        out_specs=VMEM,
        scratch_shapes=[
            pltpu.VMEM((2, width, HEAD_DIM), BF16),
            pltpu.VMEM((2, 2 * inner * count, HEAD_DIM), BF16),
            pltpu.VMEM((4, 2 * inner * count, rows), BF16),
            pltpu.SemaphoreType.DMA((3 * count,)),
        ],
        compiler_params=params(32),
        cost_estimate=SMALL,
    )(scalars, ids_own, ids_nb, gains, *ranks, normed_own, normed_nb, *pieces.arrays)


def query_kernel(count, inner, *refs):
    scalars, ids_own, ids_nb, gains, normed_own, normed_nb = refs[:6]
    ranks = refs[6:10]
    pieces = refs[10 : 10 + count]
    out_own, out_nb, weight, up, into_own, into_nb, sems = refs[10 + count :]
    deep = pieces[0].shape[0] - 2 * inner
    copies = []
    for i in range(count):
        row = pl.multiple_of(scalars[Q_ROW, i], deep)
        copies.append(
            pltpu.make_async_copy(
                pieces[i].at[pl.ds(0, deep)], weight.at[pl.ds(row, deep)], sems.at[2 * i]
            )
        )
        copies.append(
            pltpu.make_async_copy(
                pieces[i].at[pl.ds(deep, 2 * inner)],
                up.at[pl.ds(2 * inner * i, 2 * inner)],
                sems.at[2 * i + 1],
            )
        )
    for copy in copies:
        copy.start()
    spread(ranks[0][0:inner] + ranks[1][0:inner], ids_own, scalars, count, into_own)
    spread(ranks[2][0:inner] + ranks[3][0:inner], ids_nb, scalars, count, into_nb)
    for copy in copies:
        copy.wait()
    for head in range(weight.shape[1] // HEAD_DIM):
        cut = slice(head * HEAD_DIM, (head + 1) * HEAD_DIM)
        for normed, into, out in ((normed_nb, into_nb, out_nb), (normed_own, into_own, out_own)):
            block = project(normed[...], weight[:, cut], into[...], up[:, cut])
            out[:, cut] = unit(block, gains[0:1, :])


def queries_of(scalars, ids_own, ids_nb, gains, normed_own, normed_nb, ranks, pieces):
    rows, width = normed_own.shape
    count, inner = len(pieces), ranks[0].shape[0] // 3
    columns = pieces[0].shape[1]
    return pl.pallas_call(
        functools.partial(query_kernel, count, inner),
        out_shape=[jax.ShapeDtypeStruct((rows, columns), BF16)] * 2,
        in_specs=[SMEM] + [VMEM] * 9 + [ANY] * count,
        out_specs=[VMEM, VMEM],
        scratch_shapes=[
            pltpu.VMEM((width, columns), BF16),
            pltpu.VMEM((2 * inner * count, columns), BF16),
            pltpu.VMEM((2 * inner * count, rows), BF16),
            pltpu.VMEM((2 * inner * count, rows), BF16),
            pltpu.SemaphoreType.DMA((2 * count,)),
        ],
        compiler_params=params(56),
        cost_estimate=SMALL,
    )(scalars, ids_own, ids_nb, gains, normed_own, normed_nb, *ranks, *pieces)


def attend_kernel(places, queries, seg_rows, seg_keys, *refs):
    before, here_too, out, held, sems = refs
    blocks = [before.at[0], before.at[1], here_too.at[0], here_too.at[1]]
    rows = queries.shape[0]
    slots = held.shape[0]
    for wait in (False, True):
        for i in range(4):
            slot = places[i]

            @pl.when((slot >= 0) & (slot < slots))
            def _():
                copy = pltpu.make_async_copy(blocks[i], held.at[slot], sems.at[i])
                if wait:
                    copy.wait()
                else:
                    copy.start()

    tile = HEAD_DIM
    heads = queries.shape[1] // HEAD_DIM
    tiles = WINDOW // tile + 1
    per_block = rows // tile
    row = lax.broadcasted_iota(jnp.int32, (tile, tile), 0)
    column = lax.broadcasted_iota(jnp.int32, (tile, tile), 1)
    for part in range(rows // tile):
        here = slice(part * tile, (part + 1) * tile)
        query = jnp.concatenate(
            [queries[here, h * HEAD_DIM : (h + 1) * HEAD_DIM] for h in range(heads)], axis=0
        )
        total = jnp.zeros((heads * tile, 128), F32)
        summed = jnp.zeros((heads * tile, HEAD_DIM), F32)
        for step in range(tiles):
            at = part + step
            block, inside = at // per_block, at % per_block
            span = slice(inside * tile, (inside + 1) * tile)
            keys = held[block, span, 0:HEAD_DIM]
            values = held[block, span, HEAD_DIM:]
            allowed = seg_rows[here, :] == seg_keys[:, at * tile : (at + 1) * tile]
            if step == 0:
                allowed = allowed & (column > row)
            if step == tiles - 1:
                allowed = allowed & (column <= row)
            scores = lax.dot_general(
                query, keys, (((1,), (1,)), ((), ())), preferred_element_type=F32
            )
            weights = jnp.exp2(scores * (HEAD_DIM ** (-0.5) * math.log2(math.e)))
            weights = jnp.where(jnp.concatenate([allowed] * heads, axis=0), weights, 0.0)
            for cut in range(tile // 128):
                total = total + weights[:, cut * 128 : (cut + 1) * 128]
            summed = summed + jnp.dot(
                weights.astype(BF16), values, preferred_element_type=F32
            )
        result = summed / jnp.sum(total, axis=-1, keepdims=True)
        for h in range(heads):
            out[here, h * HEAD_DIM : (h + 1) * HEAD_DIM] = result[
                h * tile : (h + 1) * tile
            ].astype(BF16)


def attend(head, places, queries, seg_rows, seg_keys, blocks):
    rows = queries.shape[0]
    width = queries.shape[1] // 2
    slots = seg_keys.shape[1] // rows
    return pl.pallas_call(
        attend_kernel,
        grid=(1,),
        out_shape=jax.ShapeDtypeStruct((rows, width), BF16),
        in_specs=[
            SMEM,
            pl.BlockSpec((rows, width), lambda i: (0, head)),
            pl.BlockSpec((rows, 1), lambda i: (0, 0)),
            pl.BlockSpec((1, slots * rows), lambda i: (0, 0)),
        ]
        + [ANY] * 2,
        out_specs=pl.BlockSpec((rows, width), lambda i: (0, 0)),
        scratch_shapes=[
            pltpu.VMEM((slots, rows, 2 * HEAD_DIM), BF16),
            pltpu.SemaphoreType.DMA((4,)),
        ],
        compiler_params=params(24),
        cost_estimate=SMALL,
    )(places, queries, seg_rows, seg_keys, *blocks)


def side_kernel(count, where, *refs):
    y = where[0]
    out = refs[2 * count]
    width = refs[0].shape[1]
    for side, at in ((0, y), (1, 1 - y)):
        for i in range(count):
            start = pl.multiple_of((at * count + i) * width, width)
            out[:, pl.ds(start, width)] = refs[side * count + i][...]


def side_by_side(where, kept, got):
    rows, width = kept[0].shape
    return pl.pallas_call(
        functools.partial(side_kernel, len(kept)),
        out_shape=jax.ShapeDtypeStruct((rows, 2 * width * len(kept)), BF16),
        in_specs=[SMEM] + [VMEM] * (2 * len(kept)),
        out_specs=VMEM,
        compiler_params=params(16),
        cost_estimate=SMALL,
    )(where, *kept, *got)


def paired_body(
    residual_input,
    input_norm_gain,
    base_projection_weight,
    query_key_gains,
    adapter_down_weight,
    adapter_up_weight,
    row_adapter_index,
    row_sequence_index,
):
    rows = residual_input.shape[0]
    width_q, width_k = HEADS * HEAD_DIM, KV_HEADS * HEAD_DIM
    half_q, half_k = width_q // 2, width_k // 2
    depth = lax.axis_size("adapter") // 2
    local = adapter_down_weight.shape[0]
    deep = base_projection_weight.shape[0]
    place = lax.axis_index("dp")
    x, core = place // 2, place % 2
    owner = lax.axis_index("adapter")
    z, y = owner // 2, owner % 2
    swap_y = lambda v: route(v, depth, lambda x, c, z, y: (x, c, z, 1 - y))
    swap_x = lambda v: route(v, depth, lambda x, c, z, y: (1 - x, c, z, y))
    swap_core = lambda v: route(v, depth, lambda x, c, z, y: (x, 1 - c, z, y))
    ring = lambda v: route(v, depth, lambda x, c, z, y: (x, c, (z + 1) % depth, y))

    def onward(x, c, z, y):
        if z + 1 < depth:
            return (x, c, z + 1, y)
        after = 2 * x + c + 1
        return (after // 2, after % 2, 0, y) if after < 4 else None

    halo = lambda v: route(v, depth, onward)

    block = base_projection_weight
    top, bottom = block[: deep // 2], block[deep // 2 :]
    mine = lax.dynamic_slice_in_dim(block, y * half_k, half_k, 1)
    theirs = lax.dynamic_slice_in_dim(block, (1 - y) * half_k, half_k, 1)
    got_top = route(top, depth, lambda x, c, z, y: (0, y, z, c) if x == 0 and c != y else None)
    got_bottom = route(bottom, depth, lambda x, c, z, y: (1, y, z, c) if x == 0 else None)
    got_theirs = route(
        theirs, depth, lambda x, c, z, y: (0, c, z, 1 - y) if x == 1 else None
    )
    up_one = lax.dynamic_index_in_dim(adapter_up_weight, place, 0, keepdims=False)

    def up_half(which):
        return (
            lax.dynamic_slice_in_dim(up_one, which * half_q, half_q, 1),
            lax.dynamic_slice_in_dim(up_one, width_q + which * half_k, half_k, 1),
            lax.dynamic_slice_in_dim(up_one, width_q + width_k + which * half_k, half_k, 1),
        )

    up_other = swap_y(jnp.concatenate(up_half(1 - y), axis=1))
    share_down = lax.dynamic_index_in_dim(adapter_down_weight, place, 0, keepdims=False).T
    numbers = jnp.stack([row_adapter_index[:, 0], row_sequence_index])
    other_numbers = swap_y(numbers)
    down = [share_down, ring(share_down)]
    got_top, got_bottom, got_theirs, up_other, other_numbers, down = lax.optimization_barrier(
        (got_top, got_bottom, got_theirs, up_other, other_numbers, down)
    )
    share_q = jnp.where(x == 1, got_bottom, jnp.where(core == y, top, got_top))
    share_kv = jnp.where(x == 0, got_theirs, mine)
    up_own = jnp.concatenate(up_half(y), axis=1)
    up_pair = jnp.concatenate(
        [jnp.where(y == 0, up_own, up_other), jnp.where(y == 0, up_other, up_own)], axis=0
    )
    share_q = jnp.concatenate([share_q, up_pair[:, :half_q]], axis=0)
    share_kv = jnp.concatenate(
        [share_kv, up_pair[:, half_q : half_q + half_k], up_pair[:, half_q + half_k :]], axis=0
    )

    ids_own, ids_nb = numbers[0:1], other_numbers[0:1]
    seg_pair = jnp.where(
        y == 0,
        jnp.concatenate([numbers[1], other_numbers[1]]),
        jnp.concatenate([other_numbers[1], numbers[1]]),
    )
    normed_own = row_norm(residual_input, input_norm_gain)

    step, flip = np.arange(4).repeat(4), np.tile(np.arange(4), 4)
    chunk = (z + depth - step) % depth
    at_x = x + flip % 2 * (1 - 2 * x)
    at_core = core + flip // 2 * (1 - 2 * core)
    adapter = 2 * chunk * local + 2 * at_x + at_core
    scalars = jnp.stack(
        [
            (2 * chunk + at_core) * deep + at_x * (deep // 2),
            at_core,
            (2 * chunk + jnp.where(at_x == 1, y, 1 - y)) * deep,
            adapter,
            adapter + local,
            adapter + y * local,
        ]
    ).astype(jnp.int32)

    residual = jnp.split(residual_input, 4, axis=0)

    def group(ready, *values):
        return lax.optimization_barrier((values, ready))

    kv, q = [share_kv], [share_q]
    kv_x, kv_c, kv_xc, q_x, q_c, q_xc = [], [], [], [], [], []
    down_x, down_c, down_xc, other = [], [], [], []
    kv.append(ring(kv[0]))
    other.append(swap_y(residual[0]))
    kv_x.append(swap_x(kv[0]))
    kv_c.append(swap_core(kv[0]))
    down.append(ring(down[1]))
    down_x.append(swap_x(down[0]))
    down_c.append(swap_core(down[0]))
    for step in range(1, 4):
        (kv[step], kv_x[-1], part), _ = group((kv_c[-1],), kv[step], kv_x[-1], residual[step])
        if step < 3:
            kv.append(ring(kv[step]))
        other.append(swap_y(part))
        kv_x.append(swap_x(kv[step]))
        kv_c.append(swap_core(kv[step]))
        kv_xc.append(swap_core(kv_x[-2]))
        (onward_z, down[step], down_x[-1]), (_, other[-2]) = group(
            (down_c[-1], other[-2]),
            down[2] if step == 1 else q[-1],
            down[step],
            down_x[-1],
        )
        if step == 1:
            down[2] = onward_z
            down.append(ring(down[2]))
        else:
            q[-1] = onward_z
            q.append(ring(q[-1]))
        down_x.append(swap_x(down[step]))
        down_c.append(swap_core(down[step]))
        down_xc.append(swap_core(down_x[-2]))
    (q[0], kv_x[-1]), _ = group((kv_c[-1],), q[0], kv_x[-1])
    kv_xc.append(swap_core(kv_x[-1]))
    (down_x[-1],), (_, other[-1]) = group((down_c[-1], other[-1]), down_x[-1])
    down_xc.append(swap_core(down_x[-1]))
    def flat(*lists):
        return [piece for step in zip(*lists, strict=True) for piece in step]

    down_pieces = flat(down, down_x, down_c, down_xc)
    kv_pieces = flat(kv, kv_x, kv_c, kv_xc)
    normed_nb = row_norm(jnp.concatenate(other, axis=0), input_norm_gain)

    def tied(values, *ready):
        return lax.optimization_barrier((values, ready))[0]

    down_parts = Pieces(down_pieces, [(i, 0) for i in range(16)], down_pieces[0].shape[0])
    part_own, down_all = first_ranks(scalars, ids_own, normed_own, down_parts)
    q[2], part_own = tied((q[2], part_own))
    q.append(ring(q[2]))
    part_nb = more_ranks(scalars, ids_nb, normed_nb, down_all, 16)
    back_nb = swap_y(part_own)
    back_own = swap_y(part_nb)
    back_own, back_nb = tied((back_own, back_nb))
    gains = query_key_gains
    ranks = (part_own, back_own, part_nb, back_nb)
    kv_all = Pieces(kv_pieces, [(i, 0) for i in range(16)], kv_pieces[0].shape[0])
    kv_heads = [
        keys_values(head, scalars, ids_own, ids_nb, gains, ranks, normed_own, normed_nb, kv_all)
        for head in range(half_k // HEAD_DIM)
    ]
    seg_before = halo(seg_pair)
    q_x = [swap_x(part) for part in q[:3]]
    kv_heads[0], seg_before, q, q_x = tied((kv_heads[0], seg_before, q, q_x))
    arriving = [halo(kv_heads[0]), halo(kv_heads[1])]
    q_x.append(swap_x(q[3]))
    q, q_x[:3] = tied((q, q_x[:3]), kv_heads[1])
    q_c = [swap_core(part) for part in q]
    q_x[3], arriving[0] = tied((q_x[3], arriving[0]))
    q_xc = [swap_core(part) for part in q_x]
    q_pieces = flat(q, q_x, q_c, q_xc)
    queries_own, queries_nb = queries_of(
        scalars, ids_own, ids_nb, gains, normed_own, normed_nb, ranks, q_pieces
    )
    seg_before = jnp.where((place == 0) & (z == 0), -1, seg_before)
    seg_span = jnp.concatenate([seg_before, seg_pair])

    spans = {}
    for name, parity in (("own", y), ("nb", 1 - y)):
        seg_keys = lax.dynamic_slice_in_dim(seg_span, parity * rows, 3 * rows, 0)[None, :]
        seg_rows = lax.dynamic_slice_in_dim(seg_pair, parity * rows, rows, 0)[:, None]
        places = jnp.stack([y, 1 - y, 2 + y, 3 - y]) - parity
        spans[name] = (places.astype(jnp.int32), seg_rows, seg_keys)
    where = jnp.stack([y, place, x, core]).astype(jnp.int32)
    kept, got = [], []
    for head, both in enumerate(kv_heads):
        blocks = (tied(arriving[head], kept[-1]) if kept else arriving[head], both)
        places, seg_rows, seg_keys = spans["nb"]
        got.append(swap_y(attend(head, places, queries_nb, seg_rows, seg_keys, blocks)))
        places, seg_rows, seg_keys = spans["own"]
        kept.append(attend(head, places, queries_own, seg_rows, seg_keys, blocks))
    return side_by_side(where, kept, got)


def paired(mesh, shapes):
    residual, _, weight, _, down = shapes[:5]
    rows = residual[0] // mesh.size
    return (
        mesh.shape["dp"] == 4
        and mesh.shape["adapter"] == 8
        and down[0] // mesh.shape["adapter"] == 4
        and rows % HEAD_DIM == 0
        and 2 * rows == WINDOW
        and weight[1] == (HEADS + 2 * KV_HEADS) * HEAD_DIM
        and weight[0] // mesh.shape["adapter"] % 32 == 0
    )


def solution(mesh):
    placed = (
        P(("dp", "adapter"), None),
        P(),
        P("adapter", "dp"),
        P(),
        P("adapter", None, None),
        P("adapter", None, None),
        P(("dp", "adapter"), None),
        P(("dp", "adapter")),
    )

    def whole(*arrays):
        body = paired_body if paired(mesh, [a.shape for a in arrays]) else general_body
        return jax.shard_map(
            body, mesh=mesh, in_specs=placed, out_specs=P(("dp", "adapter"), None), check_vma=False
        )(*arrays)

    return whole
```

```python
import functools
import math

import jax
import jax.numpy as jnp
import numpy as np
from jax import lax
from jax.experimental import pallas as pl
from jax.experimental.pallas import tpu as pltpu
from jax.sharding import PartitionSpec as P

HEADS = 8
KV_HEADS = 4
HEAD_DIM = 256
WINDOW = 1024


def shifted(value, axis, by):
    size = lax.axis_size(axis)
    pairs = [(i, i + by) for i in range(size) if 0 <= i + by < size]
    return lax.ppermute(value, axis, pairs)


def head_norm(block, heads, gain):
    shaped = block.reshape(block.shape[0], heads, HEAD_DIM)
    scaled = shaped * lax.rsqrt(jnp.mean(shaped * shaped, axis=-1, keepdims=True) + 1e-06) * gain
    return scaled.astype(jnp.bfloat16)


def adapter_delta(rank_values, up_matrices):
    width_q = HEADS * HEAD_DIM
    width_k = KV_HEADS * HEAD_DIM
    inner = up_matrices.shape[1]
    part_q = jnp.einsum(
        "nacr,arq->nacq",
        rank_values[..., 0:inner],
        up_matrices[:, :, 0:width_q],
        preferred_element_type=jnp.float32,
    )
    part_k = jnp.einsum(
        "nacr,arq->nacq",
        rank_values[..., inner : 2 * inner],
        up_matrices[:, :, width_q : width_q + width_k],
        preferred_element_type=jnp.float32,
    )
    part_v = jnp.einsum(
        "nacr,arq->nacq",
        rank_values[..., 2 * inner : 3 * inner],
        up_matrices[:, :, width_q + width_k :],
        preferred_element_type=jnp.float32,
    )
    return jnp.concatenate([part_q, part_k, part_v], axis=-1).astype(jnp.bfloat16)


def adapter_ranks(adapter_slots, down_matrices):
    return jnp.einsum(
        "nacd,adr->nacr", adapter_slots, down_matrices, preferred_element_type=jnp.float32
    ).astype(jnp.bfloat16)


def general_body(
    residual_input,
    input_norm_gain,
    base_projection_weight,
    query_key_gains,
    adapter_down_weight,
    adapter_up_weight,
    row_adapter_index,
    row_sequence_index,
):
    rows = residual_input.shape[0]
    width = residual_input.shape[1]
    width_q = HEADS * HEAD_DIM
    width_k = KV_HEADS * HEAD_DIM
    group = HEADS // KV_HEADS
    values_in = residual_input.astype(jnp.float32)
    normed = (
        values_in
        * lax.rsqrt(jnp.mean(values_in * values_in, axis=-1, keepdims=True) + 1e-06)
        * input_norm_gain
    ).astype(jnp.bfloat16)
    slab = lax.all_gather(base_projection_weight, "dp", axis=1, tiled=True)
    base = jnp.dot(
        normed,
        lax.all_gather(slab, "adapter", axis=0, tiled=True),
        preferred_element_type=jnp.float32,
    ).astype(jnp.bfloat16)
    total_width = base.shape[1]
    owners = lax.axis_size("adapter")
    local_adapter_count = adapter_down_weight.shape[0]
    adapters_all = owners * local_adapter_count
    capacity = 2 * rows // adapters_all
    adapter_ids = row_adapter_index[:, 0]
    onehot = (adapter_ids[:, None] == jnp.arange(adapters_all, dtype=jnp.int32)[None, :]).astype(
        jnp.int32
    )
    earlier = jnp.cumsum(onehot, axis=0) - onehot
    place = jnp.sum(earlier * onehot, axis=1)
    slot = adapter_ids * capacity + place
    scratch_buffer = jnp.zeros((adapters_all * capacity, width), jnp.bfloat16).at[slot].set(normed)
    scratch_buffer = scratch_buffer.reshape(owners, local_adapter_count, capacity, width)
    adapter_corrections = adapter_delta(
        adapter_ranks(
            lax.all_to_all(scratch_buffer, "adapter", split_axis=0, concat_axis=0, tiled=True),
            adapter_down_weight,
        ),
        adapter_up_weight,
    )
    returned = lax.all_to_all(
        adapter_corrections, "adapter", split_axis=0, concat_axis=0, tiled=True
    )
    delta_slots = returned.reshape(adapters_all * capacity, total_width)
    delta_update = delta_slots[slot]
    projected = base.astype(jnp.float32) + delta_update.astype(jnp.float32)
    queries = head_norm(projected[:, 0:width_q], HEADS, query_key_gains[0]).reshape(
        rows, KV_HEADS, group, HEAD_DIM
    )
    keys = head_norm(
        projected[:, width_q : width_q + width_k], KV_HEADS, query_key_gains[1]
    ).reshape(rows, width_k)
    values = projected[:, width_q + width_k :].astype(jnp.bfloat16)
    before = (WINDOW + rows - 2) // rows
    key_parts = []
    value_parts = []
    seg_parts = []
    for offset in range(before, 0, -1):
        moved_keys, moved_values, moved_seg = shifted(
            (keys, values, row_sequence_index), ("dp", "adapter"), offset
        )
        key_parts.append(moved_keys)
        value_parts.append(moved_values)
        seg_parts.append(moved_seg)
    key_parts.append(keys)
    value_parts.append(values)
    seg_parts.append(row_sequence_index)
    span = (before + 1) * rows
    key_all = jnp.concatenate(key_parts, axis=0).reshape(span, KV_HEADS, HEAD_DIM)
    value_all = jnp.concatenate(value_parts, axis=0).reshape(span, KV_HEADS, HEAD_DIM)
    seg_all = jnp.concatenate(seg_parts, axis=0)
    position = lax.axis_index(("dp", "adapter"))
    query_pos = position * rows + jnp.arange(rows, dtype=jnp.int32)
    key_pos = (position - before) * rows + jnp.arange(span, dtype=jnp.int32)
    gap = query_pos[:, None] - key_pos[None, :]
    allowed = (
        (row_sequence_index[:, None] == seg_all[None, :])
        & (gap >= 0)
        & (gap < WINDOW)
        & (key_pos[None, :] >= 0)
    )
    scores = jnp.einsum(
        "tkgd,skd->kgts", queries, key_all, preferred_element_type=jnp.float32
    ) * HEAD_DIM ** (-0.5)
    weights = jnp.where(allowed[None, None], jnp.exp(scores), jnp.float32(0.0))
    total = jnp.sum(weights, axis=-1)
    probs = weights.astype(jnp.bfloat16)
    summed = jnp.einsum("kgts,skd->tkgd", probs, value_all, preferred_element_type=jnp.float32)
    result = summed / jnp.transpose(total, (2, 0, 1))[..., None]
    return result.reshape(rows, width_q).astype(jnp.bfloat16)


BF16 = jnp.bfloat16
F32 = jnp.float32
ANY = pl.BlockSpec(memory_space=pl.ANY)
SMEM = pl.BlockSpec(memory_space=pltpu.SMEM)
VMEM = pl.BlockSpec(memory_space=pltpu.VMEM)
SMALL = pl.CostEstimate(flops=1, bytes_accessed=1, transcendentals=0)
Q_ROW, KV_KIND, KV_ROW, UP_EVEN, UP_ODD, DOWN_ID = range(6)


def params(mib):
    return pltpu.CompilerParams(vmem_limit_bytes=mib << 20)


def route(value, depth, rule):
    pairs = []
    for x in range(2):
        for core in range(2):
            for z in range(depth):
                for y in range(2):
                    to = rule(x, core, z, y)
                    if to is not None:
                        source = (2 * x + core) * 2 * depth + 2 * z + y
                        pairs.append((source, (2 * to[0] + to[1]) * 2 * depth + 2 * to[2] + to[3]))
    return lax.ppermute(value, ("dp", "adapter"), pairs)


def after(value, *others):
    return lax.optimization_barrier((value, others))[0]


def row_norm(values, gain):
    values = values.astype(F32)
    scale = lax.rsqrt(jnp.mean(values * values, axis=-1, keepdims=True) + 1e-06)
    return (values * scale * gain).astype(BF16)


def copies_done(copies):
    for copy in copies:
        copy.start()
    for copy in copies:
        copy.wait()


def masked_ranks(scalars, ids, down, normed, out, count):
    deep = out.shape[0]
    every = lax.dot_general(
        down[...], normed[...], (((1,), (1,)), ((), ())), preferred_element_type=F32
    )
    total = jnp.zeros(out.shape, F32)
    for i in range(count):
        mine = ids[...] == scalars[DOWN_ID, i]
        total = total + jnp.where(mine, every[i * deep : (i + 1) * deep], 0.0)
    out[...] = total.astype(BF16)


def rank_kernel(count, scalars, ids, normed, down, first, out):
    out[0] = first[...]
    masked_ranks(scalars, ids, down, normed, out.at[1], count)


def first_rank_kernel(pieces, scalars, ids, normed, *refs):
    held = refs[: len(pieces.arrays)]
    out, down, sems = refs[len(pieces.arrays) :]
    deep, count = pieces.deep, len(pieces.names)
    copies = [
        pltpu.make_async_copy(
            pieces.cut(held, i, 0, deep), down.at[pl.ds(i * deep, deep)], sems.at[i]
        )
        for i in range(count)
    ]
    for copy in copies:
        copy.start()
    for copy in copies:
        copy.wait()
    masked_ranks(scalars, ids, down, normed, out, count)


def first_ranks(scalars, ids, normed, pieces):
    rows, width = normed.shape
    count, deep = len(pieces.names), pieces.deep
    return pl.pallas_call(
        functools.partial(first_rank_kernel, pieces),
        out_shape=[
            jax.ShapeDtypeStruct((deep, rows), BF16),
            jax.ShapeDtypeStruct((count * deep, width), BF16),
        ],
        in_specs=[SMEM, VMEM, VMEM] + [ANY] * len(pieces.arrays),
        out_specs=[VMEM, VMEM],
        scratch_shapes=[pltpu.SemaphoreType.DMA((count,))],
        compiler_params=params(24),
        cost_estimate=SMALL,
    )(scalars, ids, normed, *pieces.arrays)


def more_ranks(scalars, ids, normed, down, first, count):
    rows, width = normed.shape
    return pl.pallas_call(
        functools.partial(rank_kernel, count),
        out_shape=jax.ShapeDtypeStruct((2, down.shape[0] // count, rows), BF16),
        in_specs=[SMEM, VMEM, VMEM, VMEM, VMEM],
        out_specs=VMEM,
        compiler_params=params(24),
        cost_estimate=SMALL,
    )(scalars, ids, normed, down, first)


def spread(ranks, ids, scalars, count, into):
    inner = ranks.shape[0]
    for i in range(count):
        for odd in range(2):
            mine = ids[...] == scalars[UP_EVEN + odd, i]
            at = (2 * i + odd) * inner
            into[at : at + inner, :] = jnp.where(mine, ranks, jnp.zeros_like(ranks))


def project(normed, weight, into, up):
    base = jnp.dot(normed, weight, preferred_element_type=F32).astype(BF16)
    delta = lax.dot_general(
        into, up, (((0,), (0,)), ((), ())), preferred_element_type=F32
    ).astype(BF16)
    return base.astype(F32) + delta.astype(F32)


def unit(block, gain):
    scale = lax.rsqrt(jnp.mean(block * block, axis=-1, keepdims=True) + 1e-06)
    return (block * scale * gain).astype(BF16)


class Pieces:
    def __init__(self, arrays, names, deep):
        self.arrays, self.names, self.deep = arrays, names, deep

    def cut(self, refs, i, start, size, columns=None):
        array, at = self.names[i]
        rows = pl.ds(at * self.deep + start, size)
        return refs[array].at[rows] if columns is None else refs[array].at[rows, columns]


def kv_kernel(pieces, inner, head, *refs):
    scalars, ids_own, ids_nb, gains = refs[:4]
    ranks, ranks_there = refs[4:6]
    normed = refs[6:8]
    held = refs[8 : 8 + len(pieces.arrays)]
    out, weight, up, into, sems = refs[8 + len(pieces.arrays) :]
    deep, count = pieces.deep - 4 * inner, len(pieces.names)
    columns = pl.ds(head * HEAD_DIM, HEAD_DIM)
    copies = []
    for i in range(count):
        kind = scalars[KV_KIND, i]
        row = pl.multiple_of(scalars[KV_ROW, i], deep)
        copies.append(
            pltpu.make_async_copy(
                pieces.cut(held, i, 0, deep, columns),
                weight.at[kind, pl.ds(row, deep)],
                sems.at[3 * i],
            )
        )
        for both in range(2):
            copies.append(
                pltpu.make_async_copy(
                    pieces.cut(held, i, deep + 2 * inner * both, 2 * inner, columns),
                    up.at[both, pl.ds(2 * inner * i, 2 * inner)],
                    sems.at[3 * i + 1 + both],
                )
            )
    for copy in copies:
        copy.start()
    for side, ids in ((0, ids_own), (1, ids_nb)):
        both = ranks[side] + ranks_there[1 - side]
        for kind in range(2):
            part = both[(1 + kind) * inner : (2 + kind) * inner]
            spread(part, ids, scalars, count, into.at[2 * side + kind])
    for copy in copies:
        copy.wait()
    for side in range(2):
        keys = project(normed[side][...], weight[0], into[2 * side], up[0])
        out[side, :, 0:HEAD_DIM] = unit(keys, gains[1:2, :])
        values = project(normed[side][...], weight[1], into[2 * side + 1], up[1])
        out[side, :, HEAD_DIM:] = values.astype(BF16)


def keys_values(head, scalars, ids_own, ids_nb, gains, ranks, normed_own, normed_nb, pieces):
    rows, width = normed_own.shape
    count, inner = len(pieces.names), ranks[0].shape[1] // 3
    return pl.pallas_call(
        functools.partial(kv_kernel, pieces, inner, head),
        out_shape=jax.ShapeDtypeStruct((2, rows, 2 * HEAD_DIM), BF16),
        in_specs=[SMEM] + [VMEM] * 7 + [ANY] * len(pieces.arrays),
        out_specs=VMEM,
        scratch_shapes=[
            pltpu.VMEM((2, width, HEAD_DIM), BF16),
            pltpu.VMEM((2, 2 * inner * count, HEAD_DIM), BF16),
            pltpu.VMEM((4, 2 * inner * count, rows), BF16),
            pltpu.SemaphoreType.DMA((3 * count,)),
        ],
        compiler_params=params(32),
        cost_estimate=SMALL,
    )(scalars, ids_own, ids_nb, gains, *ranks, normed_own, normed_nb, *pieces.arrays)


def query_kernel(count, inner, head, *refs):
    scalars, ids_own, ids_nb, gains = refs[:4]
    ranks, ranks_there = refs[4:6]
    pieces = refs[8 : 8 + count]
    out, weight, up, into, normed, sems = refs[8 + count :]
    deep = pieces[0].shape[0] - 2 * inner
    columns = pl.ds(head * weight.shape[1], weight.shape[1])
    whole = [
        pltpu.make_async_copy(refs[6 + side], normed.at[side], sems.at[2 * count + side])
        for side in range(2)
    ]
    whole[0].start()
    copies = []
    for i in range(count):
        row = pl.multiple_of(scalars[Q_ROW, i], deep)
        copies.append(
            pltpu.make_async_copy(
                pieces[i].at[pl.ds(0, deep), columns],
                weight.at[pl.ds(row, deep)],
                sems.at[2 * i],
            )
        )
        copies.append(
            pltpu.make_async_copy(
                pieces[i].at[pl.ds(deep, 2 * inner), columns],
                up.at[pl.ds(2 * inner * i, 2 * inner)],
                sems.at[2 * i + 1],
            )
        )
    for copy in copies:
        copy.start()
    whole[1].start()
    for side, ids in ((0, ids_own), (1, ids_nb)):
        both = ranks[side, 0:inner] + ranks_there[1 - side, 0:inner]
        spread(both, ids, scalars, count, into.at[side])
    for copy in copies:
        copy.wait()
    for side in range(2):
        whole[side].wait()
        for at in range(weight.shape[1] // HEAD_DIM):
            cut = slice(at * HEAD_DIM, (at + 1) * HEAD_DIM)
            block = project(normed[side], weight[:, cut], into[side], up[:, cut])
            out[side, :, cut] = unit(block, gains[0:1, :])


def queries_of(head, scalars, ids_own, ids_nb, gains, ranks, normed_own, normed_nb, pieces):
    rows, width = normed_own.shape
    count, inner = len(pieces), ranks[0].shape[1] // 3
    columns = pieces[0].shape[1] // 2
    return pl.pallas_call(
        functools.partial(query_kernel, count, inner, head),
        out_shape=jax.ShapeDtypeStruct((2, rows, columns), BF16),
        in_specs=[SMEM] + [VMEM] * 5 + [ANY] * (2 + count),
        out_specs=VMEM,
        scratch_shapes=[
            pltpu.VMEM((width, columns), BF16),
            pltpu.VMEM((2 * inner * count, columns), BF16),
            pltpu.VMEM((2, 2 * inner * count, rows), BF16),
            pltpu.VMEM((2, rows, width), BF16),
            pltpu.SemaphoreType.DMA((2 * count + 2,)),
        ],
        compiler_params=params(56),
        cost_estimate=SMALL,
    )(scalars, ids_own, ids_nb, gains, *ranks, normed_own, normed_nb, *pieces)


def attend_kernel(places, queries, seg_rows, seg_keys, *refs):
    before, here_too, out, held, sems = refs
    blocks = [before.at[0], before.at[1], here_too.at[0], here_too.at[1]]
    rows = queries.shape[0]
    slots = held.shape[0]
    for wait in (False, True):
        for i in range(4):
            slot = places[i]

            @pl.when((slot >= 0) & (slot < slots))
            def _():
                copy = pltpu.make_async_copy(blocks[i], held.at[slot], sems.at[i])
                if wait:
                    copy.wait()
                else:
                    copy.start()

    tile = HEAD_DIM
    heads = queries.shape[1] // HEAD_DIM
    tiles = WINDOW // tile + 1
    per_block = rows // tile
    row = lax.broadcasted_iota(jnp.int32, (tile, tile), 0)
    column = lax.broadcasted_iota(jnp.int32, (tile, tile), 1)
    for part in range(rows // tile):
        here = slice(part * tile, (part + 1) * tile)
        query = jnp.concatenate(
            [queries[here, h * HEAD_DIM : (h + 1) * HEAD_DIM] for h in range(heads)], axis=0
        )
        total = jnp.zeros((heads * tile, 128), F32)
        summed = jnp.zeros((heads * tile, HEAD_DIM), F32)
        for step in range(tiles):
            at = part + step
            block, inside = at // per_block, at % per_block
            span = slice(inside * tile, (inside + 1) * tile)
            keys = held[block, span, 0:HEAD_DIM]
            values = held[block, span, HEAD_DIM:]
            allowed = seg_rows[here, :] == seg_keys[:, at * tile : (at + 1) * tile]
            if step == 0:
                allowed = allowed & (column > row)
            if step == tiles - 1:
                allowed = allowed & (column <= row)
            scores = lax.dot_general(
                query, keys, (((1,), (1,)), ((), ())), preferred_element_type=F32
            )
            weights = jnp.exp2(scores * (HEAD_DIM ** (-0.5) * math.log2(math.e)))
            weights = jnp.where(jnp.concatenate([allowed] * heads, axis=0), weights, 0.0)
            for cut in range(tile // 128):
                total = total + weights[:, cut * 128 : (cut + 1) * 128]
            summed = summed + jnp.dot(
                weights.astype(BF16), values, preferred_element_type=F32
            )
        result = summed / jnp.sum(total, axis=-1, keepdims=True)
        for h in range(heads):
            out[here, h * HEAD_DIM : (h + 1) * HEAD_DIM] = result[
                h * tile : (h + 1) * tile
            ].astype(BF16)


def attend(side, places, queries, seg_rows, seg_keys, blocks):
    rows, width = queries.shape[1:]
    slots = seg_keys.shape[1] // rows
    return pl.pallas_call(
        attend_kernel,
        grid=(1,),
        out_shape=jax.ShapeDtypeStruct((rows, width), BF16),
        in_specs=[
            SMEM,
            pl.BlockSpec((None, rows, width), lambda i: (side, 0, 0)),
            pl.BlockSpec((rows, 1), lambda i: (0, 0)),
            pl.BlockSpec((1, slots * rows), lambda i: (0, 0)),
        ]
        + [ANY] * 2,
        out_specs=pl.BlockSpec((rows, width), lambda i: (0, 0)),
        scratch_shapes=[
            pltpu.VMEM((slots, rows, 2 * HEAD_DIM), BF16),
            pltpu.SemaphoreType.DMA((4,)),
        ],
        compiler_params=params(24),
        cost_estimate=SMALL,
    )(places, queries, seg_rows, seg_keys, *blocks)


def side_kernel(count, where, *refs):
    y = where[0]
    out = refs[2 * count]
    width = refs[0].shape[1]
    for side, at in ((0, y), (1, 1 - y)):
        for i in range(count):
            start = pl.multiple_of((at * count + i) * width, width)
            out[:, pl.ds(start, width)] = refs[side * count + i][...]


def side_by_side(where, kept, got):
    rows, width = kept[0].shape
    return pl.pallas_call(
        functools.partial(side_kernel, len(kept)),
        out_shape=jax.ShapeDtypeStruct((rows, 2 * width * len(kept)), BF16),
        in_specs=[SMEM] + [VMEM] * (2 * len(kept)),
        out_specs=VMEM,
        compiler_params=params(16),
        cost_estimate=SMALL,
    )(where, *kept, *got)


def paired_body(
    residual_input,
    input_norm_gain,
    base_projection_weight,
    query_key_gains,
    adapter_down_weight,
    adapter_up_weight,
    row_adapter_index,
    row_sequence_index,
):
    rows = residual_input.shape[0]
    width_q, width_k = HEADS * HEAD_DIM, KV_HEADS * HEAD_DIM
    half_q, half_k = width_q // 2, width_k // 2
    depth = lax.axis_size("adapter") // 2
    local = adapter_down_weight.shape[0]
    deep = base_projection_weight.shape[0]
    place = lax.axis_index("dp")
    x, core = place // 2, place % 2
    owner = lax.axis_index("adapter")
    z, y = owner // 2, owner % 2
    swap_y = lambda v: route(v, depth, lambda x, c, z, y: (x, c, z, 1 - y))
    swap_x = lambda v: route(v, depth, lambda x, c, z, y: (1 - x, c, z, y))
    swap_core = lambda v: route(v, depth, lambda x, c, z, y: (x, 1 - c, z, y))
    ring = lambda v: route(v, depth, lambda x, c, z, y: (x, c, (z + 1) % depth, y))

    def onward(x, c, z, y):
        if z + 1 < depth:
            return (x, c, z + 1, y)
        after = 2 * x + c + 1
        return (after // 2, after % 2, 0, y) if after < 4 else None

    halo = lambda v: route(v, depth, onward)

    block = base_projection_weight
    top, bottom = block[: deep // 2], block[deep // 2 :]
    mine = lax.dynamic_slice_in_dim(block, y * half_k, half_k, 1)
    theirs = lax.dynamic_slice_in_dim(block, (1 - y) * half_k, half_k, 1)
    got_top = route(top, depth, lambda x, c, z, y: (0, y, z, c) if x == 0 and c != y else None)
    got_bottom = route(bottom, depth, lambda x, c, z, y: (1, y, z, c) if x == 0 else None)
    got_theirs = route(
        theirs, depth, lambda x, c, z, y: (0, c, z, 1 - y) if x == 1 else None
    )
    up_one = lax.dynamic_index_in_dim(adapter_up_weight, place, 0, keepdims=False)

    def up_half(which):
        return (
            lax.dynamic_slice_in_dim(up_one, which * half_q, half_q, 1),
            lax.dynamic_slice_in_dim(up_one, width_q + which * half_k, half_k, 1),
            lax.dynamic_slice_in_dim(up_one, width_q + width_k + which * half_k, half_k, 1),
        )

    up_other = swap_y(jnp.concatenate(up_half(1 - y), axis=1))
    share_down = lax.dynamic_index_in_dim(adapter_down_weight, place, 0, keepdims=False).T
    numbers = jnp.stack([row_adapter_index[:, 0], row_sequence_index])
    other_numbers = swap_y(numbers)
    down = [share_down, ring(share_down)]
    got_top, got_bottom, got_theirs, up_other, other_numbers, down = lax.optimization_barrier(
        (got_top, got_bottom, got_theirs, up_other, other_numbers, down)
    )
    share_q = jnp.where(x == 1, got_bottom, jnp.where(core == y, top, got_top))
    share_kv = jnp.where(x == 0, got_theirs, mine)
    up_own = jnp.concatenate(up_half(y), axis=1)
    up_pair = jnp.concatenate(
        [jnp.where(y == 0, up_own, up_other), jnp.where(y == 0, up_other, up_own)], axis=0
    )
    share_q = jnp.concatenate([share_q, up_pair[:, :half_q]], axis=0)
    share_kv = jnp.concatenate(
        [share_kv, up_pair[:, half_q : half_q + half_k], up_pair[:, half_q + half_k :]], axis=0
    )

    ids_own, ids_nb = numbers[0:1], other_numbers[0:1]
    seg_pair = jnp.where(
        y == 0,
        jnp.concatenate([numbers[1], other_numbers[1]]),
        jnp.concatenate([other_numbers[1], numbers[1]]),
    )
    normed_own = row_norm(residual_input, input_norm_gain)

    step, flip = np.arange(4).repeat(4), np.tile(np.arange(4), 4)
    chunk = (z + depth - step) % depth
    at_x = x + flip % 2 * (1 - 2 * x)
    at_core = core + flip // 2 * (1 - 2 * core)
    adapter = 2 * chunk * local + 2 * at_x + at_core
    scalars = jnp.stack(
        [
            (2 * chunk + at_core) * deep + at_x * (deep // 2),
            at_core,
            (2 * chunk + jnp.where(at_x == 1, y, 1 - y)) * deep,
            adapter,
            adapter + local,
            adapter + y * local,
        ]
    ).astype(jnp.int32)

    residual = jnp.split(residual_input, 4, axis=0)

    def group(ready, *values):
        return lax.optimization_barrier((values, ready))

    kv, q = [share_kv], [share_q]
    kv_x, kv_c, kv_xc, q_x, q_c, q_xc = [], [], [], [], [], []
    down_x, down_c, down_xc, other = [], [], [], []
    kv.append(ring(kv[0]))
    other.append(swap_y(residual[0]))
    kv_x.append(swap_x(kv[0]))
    kv_c.append(swap_core(kv[0]))
    down.append(ring(down[1]))
    down_x.append(swap_x(down[0]))
    down_c.append(swap_core(down[0]))
    for step in range(1, 4):
        (kv[step], kv_x[-1], part), _ = group((kv_c[-1],), kv[step], kv_x[-1], residual[step])
        if step < 3:
            kv.append(ring(kv[step]))
        other.append(swap_y(part))
        kv_x.append(swap_x(kv[step]))
        kv_c.append(swap_core(kv[step]))
        kv_xc.append(swap_core(kv_x[-2]))
        (onward_z, down[step], down_x[-1]), (_, other[-2]) = group(
            (down_c[-1], other[-2]),
            down[2] if step == 1 else q[-1],
            down[step],
            down_x[-1],
        )
        if step == 1:
            down[2] = onward_z
            down.append(ring(down[2]))
        else:
            q[-1] = onward_z
            q.append(ring(q[-1]))
        down_x.append(swap_x(down[step]))
        down_c.append(swap_core(down[step]))
        down_xc.append(swap_core(down_x[-2]))
    (q[0], kv_x[-1]), _ = group((kv_c[-1],), q[0], kv_x[-1])
    kv_xc.append(swap_core(kv_x[-1]))
    (down_x[-1],), (_, other[-1]) = group((down_c[-1], other[-1]), down_x[-1])
    down_xc.append(swap_core(down_x[-1]))
    def flat(*lists):
        return [piece for step in zip(*lists, strict=True) for piece in step]

    down_pieces = flat(down, down_x, down_c, down_xc)
    kv_pieces = flat(kv, kv_x, kv_c, kv_xc)
    normed_nb = row_norm(jnp.concatenate(other, axis=0), input_norm_gain)

    def tied(values, *ready):
        return lax.optimization_barrier((values, ready))[0]

    down_parts = Pieces(down_pieces, [(i, 0) for i in range(16)], down_pieces[0].shape[0])
    part_own, down_all = first_ranks(scalars, ids_own, normed_own, down_parts)
    q[2], part_own = tied((q[2], part_own))
    q.append(ring(q[2]))
    ranks_here = more_ranks(scalars, ids_nb, normed_nb, down_all, part_own, 16)
    ranks = (ranks_here, swap_y(ranks_here))
    gains = query_key_gains
    kv_all = Pieces(kv_pieces, [(i, 0) for i in range(16)], kv_pieces[0].shape[0])
    kv_heads = [
        keys_values(head, scalars, ids_own, ids_nb, gains, ranks, normed_own, normed_nb, kv_all)
        for head in range(half_k // HEAD_DIM)
    ]
    seg_before = halo(seg_pair)
    q_x = [swap_x(part) for part in q[:3]]
    kv_heads[0], seg_before, q, q_x[:2] = tied((kv_heads[0], seg_before, q, q_x[:2]))
    arriving = [halo(kv_heads[0]), halo(kv_heads[1])]
    q_x.append(swap_x(q[3]))
    q, q_x[:3] = tied((q, q_x[:3]), kv_heads[1])
    q_c = [swap_core(part) for part in q]
    q_xc = [swap_core(part) for part in q_x[:3]]
    q_x[3], arriving[0], q_c, q_xc = tied((q_x[3], arriving[0], q_c, q_xc))
    q_xc.append(swap_core(q_x[3]))
    q_pieces = flat(q, q_x, q_c, q_xc)
    project_queries = lambda head, ranks: queries_of(
        head, scalars, ids_own, ids_nb, gains, ranks, normed_own, normed_nb, q_pieces
    )
    seg_before = jnp.where((place == 0) & (z == 0), -1, seg_before)
    seg_span = jnp.concatenate([seg_before, seg_pair])

    spans = {}
    for name, parity in (("own", y), ("nb", 1 - y)):
        seg_keys = lax.dynamic_slice_in_dim(seg_span, parity * rows, 3 * rows, 0)[None, :]
        seg_rows = lax.dynamic_slice_in_dim(seg_pair, parity * rows, rows, 0)[:, None]
        places = jnp.stack([y, 1 - y, 2 + y, 3 - y]) - parity
        spans[name] = (places.astype(jnp.int32), seg_rows, seg_keys)
    where = jnp.stack([y, place, x, core]).astype(jnp.int32)
    kept, got, queries, last = [], [], [], ranks
    for head, both in enumerate(kv_heads):
        queries.append(project_queries(head, last))
        places, seg_rows, seg_keys = spans["nb"]
        sent = attend(1, places, queries[head], seg_rows, seg_keys, (arriving[head], both))
        got.append(swap_y(sent))
        last = tied(ranks, sent)
    for head, both in enumerate(kv_heads):
        places, seg_rows, seg_keys = spans["own"]
        mine = tied(queries[head], last)
        kept.append(attend(0, places, mine, seg_rows, seg_keys, (arriving[head], both)))
    return side_by_side(where, kept, got)


def paired(mesh, shapes):
    residual, _, weight, _, down = shapes[:5]
    rows = residual[0] // mesh.size
    return (
        mesh.shape["dp"] == 4
        and mesh.shape["adapter"] == 8
        and down[0] // mesh.shape["adapter"] == 4
        and rows % HEAD_DIM == 0
        and 2 * rows == WINDOW
        and weight[1] == (HEADS + 2 * KV_HEADS) * HEAD_DIM
        and weight[0] // mesh.shape["adapter"] % 32 == 0
    )


def solution(mesh):
    placed = (
        P(("dp", "adapter"), None),
        P(),
        P("adapter", "dp"),
        P(),
        P("adapter", None, None),
        P("adapter", None, None),
        P(("dp", "adapter"), None),
        P(("dp", "adapter")),
    )

    def whole(*arrays):
        body = paired_body if paired(mesh, [a.shape for a in arrays]) else general_body
        return jax.shard_map(
            body, mesh=mesh, in_specs=placed, out_specs=P(("dp", "adapter"), None), check_vma=False
        )(*arrays)

    return whole
```

```python
import functools
import math

import jax
import jax.numpy as jnp
import numpy as np
from jax import lax
from jax.experimental import pallas as pl
from jax.experimental.pallas import tpu as pltpu
from jax.sharding import PartitionSpec as P

HEADS = 8
KV_HEADS = 4
HEAD_DIM = 256
WINDOW = 1024


def shifted(value, axis, by):
    size = lax.axis_size(axis)
    pairs = [(i, i + by) for i in range(size) if 0 <= i + by < size]
    return lax.ppermute(value, axis, pairs)


def head_norm(block, heads, gain):
    shaped = block.reshape(block.shape[0], heads, HEAD_DIM)
    scaled = shaped * lax.rsqrt(jnp.mean(shaped * shaped, axis=-1, keepdims=True) + 1e-06) * gain
    return scaled.astype(jnp.bfloat16)


def adapter_delta(rank_values, up_matrices):
    width_q = HEADS * HEAD_DIM
    width_k = KV_HEADS * HEAD_DIM
    inner = up_matrices.shape[1]
    part_q = jnp.einsum(
        "nacr,arq->nacq",
        rank_values[..., 0:inner],
        up_matrices[:, :, 0:width_q],
        preferred_element_type=jnp.float32,
    )
    part_k = jnp.einsum(
        "nacr,arq->nacq",
        rank_values[..., inner : 2 * inner],
        up_matrices[:, :, width_q : width_q + width_k],
        preferred_element_type=jnp.float32,
    )
    part_v = jnp.einsum(
        "nacr,arq->nacq",
        rank_values[..., 2 * inner : 3 * inner],
        up_matrices[:, :, width_q + width_k :],
        preferred_element_type=jnp.float32,
    )
    return jnp.concatenate([part_q, part_k, part_v], axis=-1).astype(jnp.bfloat16)


def adapter_ranks(adapter_slots, down_matrices):
    return jnp.einsum(
        "nacd,adr->nacr", adapter_slots, down_matrices, preferred_element_type=jnp.float32
    ).astype(jnp.bfloat16)


def general_body(
    residual_input,
    input_norm_gain,
    base_projection_weight,
    query_key_gains,
    adapter_down_weight,
    adapter_up_weight,
    row_adapter_index,
    row_sequence_index,
):
    rows = residual_input.shape[0]
    width = residual_input.shape[1]
    width_q = HEADS * HEAD_DIM
    width_k = KV_HEADS * HEAD_DIM
    group = HEADS // KV_HEADS
    values_in = residual_input.astype(jnp.float32)
    normed = (
        values_in
        * lax.rsqrt(jnp.mean(values_in * values_in, axis=-1, keepdims=True) + 1e-06)
        * input_norm_gain
    ).astype(jnp.bfloat16)
    slab = lax.all_gather(base_projection_weight, "dp", axis=1, tiled=True)
    base = jnp.dot(
        normed,
        lax.all_gather(slab, "adapter", axis=0, tiled=True),
        preferred_element_type=jnp.float32,
    ).astype(jnp.bfloat16)
    total_width = base.shape[1]
    owners = lax.axis_size("adapter")
    local_adapter_count = adapter_down_weight.shape[0]
    adapters_all = owners * local_adapter_count
    capacity = 2 * rows // adapters_all
    adapter_ids = row_adapter_index[:, 0]
    onehot = (adapter_ids[:, None] == jnp.arange(adapters_all, dtype=jnp.int32)[None, :]).astype(
        jnp.int32
    )
    earlier = jnp.cumsum(onehot, axis=0) - onehot
    place = jnp.sum(earlier * onehot, axis=1)
    slot = adapter_ids * capacity + place
    scratch_buffer = jnp.zeros((adapters_all * capacity, width), jnp.bfloat16).at[slot].set(normed)
    scratch_buffer = scratch_buffer.reshape(owners, local_adapter_count, capacity, width)
    adapter_corrections = adapter_delta(
        adapter_ranks(
            lax.all_to_all(scratch_buffer, "adapter", split_axis=0, concat_axis=0, tiled=True),
            adapter_down_weight,
        ),
        adapter_up_weight,
    )
    returned = lax.all_to_all(
        adapter_corrections, "adapter", split_axis=0, concat_axis=0, tiled=True
    )
    delta_slots = returned.reshape(adapters_all * capacity, total_width)
    delta_update = delta_slots[slot]
    projected = base.astype(jnp.float32) + delta_update.astype(jnp.float32)
    queries = head_norm(projected[:, 0:width_q], HEADS, query_key_gains[0]).reshape(
        rows, KV_HEADS, group, HEAD_DIM
    )
    keys = head_norm(
        projected[:, width_q : width_q + width_k], KV_HEADS, query_key_gains[1]
    ).reshape(rows, width_k)
    values = projected[:, width_q + width_k :].astype(jnp.bfloat16)
    before = (WINDOW + rows - 2) // rows
    key_parts = []
    value_parts = []
    seg_parts = []
    for offset in range(before, 0, -1):
        moved_keys, moved_values, moved_seg = shifted(
            (keys, values, row_sequence_index), ("dp", "adapter"), offset
        )
        key_parts.append(moved_keys)
        value_parts.append(moved_values)
        seg_parts.append(moved_seg)
    key_parts.append(keys)
    value_parts.append(values)
    seg_parts.append(row_sequence_index)
    span = (before + 1) * rows
    key_all = jnp.concatenate(key_parts, axis=0).reshape(span, KV_HEADS, HEAD_DIM)
    value_all = jnp.concatenate(value_parts, axis=0).reshape(span, KV_HEADS, HEAD_DIM)
    seg_all = jnp.concatenate(seg_parts, axis=0)
    position = lax.axis_index(("dp", "adapter"))
    query_pos = position * rows + jnp.arange(rows, dtype=jnp.int32)
    key_pos = (position - before) * rows + jnp.arange(span, dtype=jnp.int32)
    gap = query_pos[:, None] - key_pos[None, :]
    allowed = (
        (row_sequence_index[:, None] == seg_all[None, :])
        & (gap >= 0)
        & (gap < WINDOW)
        & (key_pos[None, :] >= 0)
    )
    scores = jnp.einsum(
        "tkgd,skd->kgts", queries, key_all, preferred_element_type=jnp.float32
    ) * HEAD_DIM ** (-0.5)
    weights = jnp.where(allowed[None, None], jnp.exp(scores), jnp.float32(0.0))
    total = jnp.sum(weights, axis=-1)
    probs = weights.astype(jnp.bfloat16)
    summed = jnp.einsum("kgts,skd->tkgd", probs, value_all, preferred_element_type=jnp.float32)
    result = summed / jnp.transpose(total, (2, 0, 1))[..., None]
    return result.reshape(rows, width_q).astype(jnp.bfloat16)


BF16 = jnp.bfloat16
F32 = jnp.float32
ANY = pl.BlockSpec(memory_space=pl.ANY)
SMEM = pl.BlockSpec(memory_space=pltpu.SMEM)
VMEM = pl.BlockSpec(memory_space=pltpu.VMEM)
SMALL = pl.CostEstimate(flops=1, bytes_accessed=1, transcendentals=0)
Q_ROW, KV_KIND, KV_ROW, UP_EVEN, UP_ODD, DOWN_ID = range(6)


def params(mib):
    return pltpu.CompilerParams(vmem_limit_bytes=mib << 20)


def route(value, depth, rule):
    pairs = []
    for x in range(2):
        for core in range(2):
            for z in range(depth):
                for y in range(2):
                    to = rule(x, core, z, y)
                    if to is not None:
                        source = (2 * x + core) * 2 * depth + 2 * z + y
                        pairs.append((source, (2 * to[0] + to[1]) * 2 * depth + 2 * to[2] + to[3]))
    return lax.ppermute(value, ("dp", "adapter"), pairs)


def after(value, *others):
    return lax.optimization_barrier((value, others))[0]


def row_norm(values, gain):
    values = values.astype(F32)
    scale = lax.rsqrt(jnp.mean(values * values, axis=-1, keepdims=True) + 1e-06)
    return (values * scale * gain).astype(BF16)


def copies_done(copies):
    for copy in copies:
        copy.start()
    for copy in copies:
        copy.wait()


def masked_ranks(scalars, ids, down, normed, out, count, waits=((),)):
    deep, share = out.shape[0], count // len(waits)
    total = jnp.zeros(out.shape, F32)
    for part, copies in enumerate(waits):
        for copy in copies:
            copy.wait()
        every = lax.dot_general(
            down[part * share * deep : (part + 1) * share * deep],
            normed[...],
            (((1,), (1,)), ((), ())),
            preferred_element_type=F32,
        )
        for i in range(share):
            mine = ids[...] == scalars[DOWN_ID, part * share + i]
            total = total + jnp.where(mine, every[i * deep : (i + 1) * deep], 0.0)
    out[...] = total.astype(BF16)


def rank_kernel(count, scalars, ids, normed, down, first, out):
    out[0] = first[...]
    masked_ranks(scalars, ids, down, normed, out.at[1], count)


def first_rank_kernel(pieces, scalars, ids, normed, *refs):
    held = refs[: len(pieces.arrays)]
    out, down, sems = refs[len(pieces.arrays) :]
    deep, count = pieces.deep, len(pieces.names)
    copies = [
        pltpu.make_async_copy(
            pieces.cut(held, i, 0, deep), down.at[pl.ds(i * deep, deep)], sems.at[i]
        )
        for i in range(count)
    ]
    for copy in copies:
        copy.start()
    masked_ranks(scalars, ids, down, normed, out, count, (copies[: count // 2], copies[count // 2 :]))


def first_ranks(scalars, ids, normed, pieces):
    rows, width = normed.shape
    count, deep = len(pieces.names), pieces.deep
    return pl.pallas_call(
        functools.partial(first_rank_kernel, pieces),
        out_shape=[
            jax.ShapeDtypeStruct((deep, rows), BF16),
            jax.ShapeDtypeStruct((count * deep, width), BF16),
        ],
        in_specs=[SMEM, VMEM, VMEM] + [ANY] * len(pieces.arrays),
        out_specs=[VMEM, VMEM],
        scratch_shapes=[pltpu.SemaphoreType.DMA((count,))],
        compiler_params=params(24),
        cost_estimate=SMALL,
    )(scalars, ids, normed, *pieces.arrays)


def more_ranks(scalars, ids, normed, down, first, count):
    rows, width = normed.shape
    return pl.pallas_call(
        functools.partial(rank_kernel, count),
        out_shape=jax.ShapeDtypeStruct((2, down.shape[0] // count, rows), BF16),
        in_specs=[SMEM, VMEM, VMEM, VMEM, VMEM],
        out_specs=VMEM,
        compiler_params=params(24),
        cost_estimate=SMALL,
    )(scalars, ids, normed, down, first)


def spread(ranks, ids, scalars, count, into):
    inner = ranks.shape[0]
    for i in range(count):
        for odd in range(2):
            mine = ids[...] == scalars[UP_EVEN + odd, i]
            at = (2 * i + odd) * inner
            into[at : at + inner, :] = jnp.where(mine, ranks, jnp.zeros_like(ranks))


def project(normed, weight, into, up):
    base = jnp.dot(normed, weight, preferred_element_type=F32).astype(BF16)
    delta = lax.dot_general(
        into, up, (((0,), (0,)), ((), ())), preferred_element_type=F32
    ).astype(BF16)
    return base.astype(F32) + delta.astype(F32)


def unit(block, gain):
    scale = lax.rsqrt(jnp.mean(block * block, axis=-1, keepdims=True) + 1e-06)
    return (block * scale * gain).astype(BF16)


class Pieces:
    def __init__(self, arrays, names, deep):
        self.arrays, self.names, self.deep = arrays, names, deep

    def cut(self, refs, i, start, size, columns=None):
        array, at = self.names[i]
        rows = pl.ds(at * self.deep + start, size)
        return refs[array].at[rows] if columns is None else refs[array].at[rows, columns]


def kv_kernel(pieces, inner, head, *refs):
    scalars, ids_own, ids_nb, gains = refs[:4]
    ranks, ranks_there = refs[4:6]
    normed = refs[6:8]
    held = refs[8 : 8 + len(pieces.arrays)]
    out, weight, up, into, sems = refs[8 + len(pieces.arrays) :]
    deep, count = pieces.deep - 4 * inner, len(pieces.names)
    columns = pl.ds(head * HEAD_DIM, HEAD_DIM)
    copies = []
    for i in range(count):
        kind = scalars[KV_KIND, i]
        row = pl.multiple_of(scalars[KV_ROW, i], deep)
        copies.append(
            pltpu.make_async_copy(
                pieces.cut(held, i, 0, deep, columns),
                weight.at[kind, pl.ds(row, deep)],
                sems.at[3 * i],
            )
        )
        for both in range(2):
            copies.append(
                pltpu.make_async_copy(
                    pieces.cut(held, i, deep + 2 * inner * both, 2 * inner, columns),
                    up.at[both, pl.ds(2 * inner * i, 2 * inner)],
                    sems.at[3 * i + 1 + both],
                )
            )
    for copy in copies:
        copy.start()
    for side, ids in ((0, ids_own), (1, ids_nb)):
        both = ranks[side] + ranks_there[1 - side]
        for kind in range(2):
            part = both[(1 + kind) * inner : (2 + kind) * inner]
            spread(part, ids, scalars, count, into.at[2 * side + kind])
    for copy in copies:
        copy.wait()
    for side in range(2):
        keys = project(normed[side][...], weight[0], into[2 * side], up[0])
        out[side, :, 0:HEAD_DIM] = unit(keys, gains[1:2, :])
        values = project(normed[side][...], weight[1], into[2 * side + 1], up[1])
        out[side, :, HEAD_DIM:] = values.astype(BF16)


def keys_values(head, scalars, ids_own, ids_nb, gains, ranks, normed_own, normed_nb, pieces):
    rows, width = normed_own.shape
    count, inner = len(pieces.names), ranks[0].shape[1] // 3
    return pl.pallas_call(
        functools.partial(kv_kernel, pieces, inner, head),
        out_shape=jax.ShapeDtypeStruct((2, rows, 2 * HEAD_DIM), BF16),
        in_specs=[SMEM] + [VMEM] * 7 + [ANY] * len(pieces.arrays),
        out_specs=VMEM,
        scratch_shapes=[
            pltpu.VMEM((2, width, HEAD_DIM), BF16),
            pltpu.VMEM((2, 2 * inner * count, HEAD_DIM), BF16),
            pltpu.VMEM((4, 2 * inner * count, rows), BF16),
            pltpu.SemaphoreType.DMA((3 * count,)),
        ],
        compiler_params=params(32),
        cost_estimate=SMALL,
    )(scalars, ids_own, ids_nb, gains, *ranks, normed_own, normed_nb, *pieces.arrays)


def query_kernel(count, inner, head, *refs):
    scalars, ids_own, ids_nb, gains = refs[:4]
    ranks, ranks_there = refs[4:6]
    pieces = refs[8 : 8 + count]
    out, weight, up, into, normed, sems = refs[8 + count :]
    deep = pieces[0].shape[0] - 2 * inner
    columns = pl.ds(head * weight.shape[1], weight.shape[1])
    whole = [
        pltpu.make_async_copy(refs[6 + side], normed.at[side], sems.at[2 * count + side])
        for side in range(2)
    ]
    whole[0].start()
    copies = []
    for i in range(count):
        row = pl.multiple_of(scalars[Q_ROW, i], deep)
        copies.append(
            pltpu.make_async_copy(
                pieces[i].at[pl.ds(0, deep), columns],
                weight.at[pl.ds(row, deep)],
                sems.at[2 * i],
            )
        )
        copies.append(
            pltpu.make_async_copy(
                pieces[i].at[pl.ds(deep, 2 * inner), columns],
                up.at[pl.ds(2 * inner * i, 2 * inner)],
                sems.at[2 * i + 1],
            )
        )
    for copy in copies:
        copy.start()
    whole[1].start()
    for side, ids in ((0, ids_own), (1, ids_nb)):
        both = ranks[side, 0:inner] + ranks_there[1 - side, 0:inner]
        spread(both, ids, scalars, count, into.at[side])
    for copy in copies:
        copy.wait()
    for side in range(2):
        whole[side].wait()
        for at in range(weight.shape[1] // HEAD_DIM):
            cut = slice(at * HEAD_DIM, (at + 1) * HEAD_DIM)
            block = project(normed[side], weight[:, cut], into[side], up[:, cut])
            out[side, :, cut] = unit(block, gains[0:1, :])


def queries_of(head, scalars, ids_own, ids_nb, gains, ranks, normed_own, normed_nb, pieces):
    rows, width = normed_own.shape
    count, inner = len(pieces), ranks[0].shape[1] // 3
    columns = pieces[0].shape[1] // 2
    return pl.pallas_call(
        functools.partial(query_kernel, count, inner, head),
        out_shape=jax.ShapeDtypeStruct((2, rows, columns), BF16),
        in_specs=[SMEM] + [VMEM] * 5 + [ANY] * (2 + count),
        out_specs=VMEM,
        scratch_shapes=[
            pltpu.VMEM((width, columns), BF16),
            pltpu.VMEM((2 * inner * count, columns), BF16),
            pltpu.VMEM((2, 2 * inner * count, rows), BF16),
            pltpu.VMEM((2, rows, width), BF16),
            pltpu.SemaphoreType.DMA((2 * count + 2,)),
        ],
        compiler_params=params(56),
        cost_estimate=SMALL,
    )(scalars, ids_own, ids_nb, gains, *ranks, normed_own, normed_nb, *pieces)


def attend_kernel(places, queries, seg_rows, seg_keys, *refs):
    before, here_too, out, held, sems = refs
    blocks = [before.at[0], before.at[1], here_too.at[0], here_too.at[1]]
    rows = queries.shape[0]
    slots = held.shape[0]
    for wait in (False, True):
        for i in range(4):
            slot = places[i]

            @pl.when((slot >= 0) & (slot < slots))
            def _():
                copy = pltpu.make_async_copy(blocks[i], held.at[slot], sems.at[i])
                if wait:
                    copy.wait()
                else:
                    copy.start()

    tile = HEAD_DIM
    heads = queries.shape[1] // HEAD_DIM
    tiles = WINDOW // tile + 1
    per_block = rows // tile
    row = lax.broadcasted_iota(jnp.int32, (tile, tile), 0)
    column = lax.broadcasted_iota(jnp.int32, (tile, tile), 1)
    for part in range(rows // tile):
        here = slice(part * tile, (part + 1) * tile)
        query = jnp.concatenate(
            [queries[here, h * HEAD_DIM : (h + 1) * HEAD_DIM] for h in range(heads)], axis=0
        )
        total = jnp.zeros((heads * tile, 128), F32)
        summed = jnp.zeros((heads * tile, HEAD_DIM), F32)
        for step in range(tiles):
            at = part + step
            block, inside = at // per_block, at % per_block
            span = slice(inside * tile, (inside + 1) * tile)
            keys = held[block, span, 0:HEAD_DIM]
            values = held[block, span, HEAD_DIM:]
            allowed = seg_rows[here, :] == seg_keys[:, at * tile : (at + 1) * tile]
            if step == 0:
                allowed = allowed & (column > row)
            if step == tiles - 1:
                allowed = allowed & (column <= row)
            scores = lax.dot_general(
                query, keys, (((1,), (1,)), ((), ())), preferred_element_type=F32
            )
            weights = jnp.exp2(scores * (HEAD_DIM ** (-0.5) * math.log2(math.e)))
            weights = jnp.where(jnp.concatenate([allowed] * heads, axis=0), weights, 0.0)
            for cut in range(tile // 128):
                total = total + weights[:, cut * 128 : (cut + 1) * 128]
            summed = summed + jnp.dot(
                weights.astype(BF16), values, preferred_element_type=F32
            )
        result = summed / jnp.sum(total, axis=-1, keepdims=True)
        for h in range(heads):
            out[here, h * HEAD_DIM : (h + 1) * HEAD_DIM] = result[
                h * tile : (h + 1) * tile
            ].astype(BF16)


def attend(side, places, queries, seg_rows, seg_keys, blocks):
    rows, width = queries.shape[1:]
    slots = seg_keys.shape[1] // rows
    return pl.pallas_call(
        attend_kernel,
        grid=(1,),
        out_shape=jax.ShapeDtypeStruct((rows, width), BF16),
        in_specs=[
            SMEM,
            pl.BlockSpec((None, rows, width), lambda i: (side, 0, 0)),
            pl.BlockSpec((rows, 1), lambda i: (0, 0)),
            pl.BlockSpec((1, slots * rows), lambda i: (0, 0)),
        ]
        + [ANY] * 2,
        out_specs=pl.BlockSpec((rows, width), lambda i: (0, 0)),
        scratch_shapes=[
            pltpu.VMEM((slots, rows, 2 * HEAD_DIM), BF16),
            pltpu.SemaphoreType.DMA((4,)),
        ],
        compiler_params=params(24),
        cost_estimate=SMALL,
    )(places, queries, seg_rows, seg_keys, *blocks)


def side_kernel(count, where, *refs):
    y = where[0]
    out = refs[2 * count]
    width = refs[0].shape[1]
    for side, at in ((0, y), (1, 1 - y)):
        for i in range(count):
            start = pl.multiple_of((at * count + i) * width, width)
            out[:, pl.ds(start, width)] = refs[side * count + i][...]


def side_by_side(where, kept, got):
    rows, width = kept[0].shape
    return pl.pallas_call(
        functools.partial(side_kernel, len(kept)),
        out_shape=jax.ShapeDtypeStruct((rows, 2 * width * len(kept)), BF16),
        in_specs=[SMEM] + [VMEM] * (2 * len(kept)),
        out_specs=VMEM,
        compiler_params=params(16),
        cost_estimate=SMALL,
    )(where, *kept, *got)


def paired_body(
    residual_input,
    input_norm_gain,
    base_projection_weight,
    query_key_gains,
    adapter_down_weight,
    adapter_up_weight,
    row_adapter_index,
    row_sequence_index,
):
    rows = residual_input.shape[0]
    width_q, width_k = HEADS * HEAD_DIM, KV_HEADS * HEAD_DIM
    half_q, half_k = width_q // 2, width_k // 2
    depth = lax.axis_size("adapter") // 2
    local = adapter_down_weight.shape[0]
    deep = base_projection_weight.shape[0]
    place = lax.axis_index("dp")
    x, core = place // 2, place % 2
    owner = lax.axis_index("adapter")
    z, y = owner // 2, owner % 2
    swap_y = lambda v: route(v, depth, lambda x, c, z, y: (x, c, z, 1 - y))
    swap_x = lambda v: route(v, depth, lambda x, c, z, y: (1 - x, c, z, y))
    swap_core = lambda v: route(v, depth, lambda x, c, z, y: (x, 1 - c, z, y))
    ring = lambda v: route(v, depth, lambda x, c, z, y: (x, c, (z + 1) % depth, y))

    def onward(x, c, z, y):
        if z + 1 < depth:
            return (x, c, z + 1, y)
        after = 2 * x + c + 1
        return (after // 2, after % 2, 0, y) if after < 4 else None

    halo = lambda v: route(v, depth, onward)

    block = base_projection_weight
    top, bottom = block[: deep // 2], block[deep // 2 :]
    mine = lax.dynamic_slice_in_dim(block, y * half_k, half_k, 1)
    theirs = lax.dynamic_slice_in_dim(block, (1 - y) * half_k, half_k, 1)
    got_top = route(top, depth, lambda x, c, z, y: (0, y, z, c) if x == 0 and c != y else None)
    got_bottom = route(bottom, depth, lambda x, c, z, y: (1, y, z, c) if x == 0 else None)
    got_theirs = route(
        theirs, depth, lambda x, c, z, y: (0, c, z, 1 - y) if x == 1 else None
    )
    up_one = lax.dynamic_index_in_dim(adapter_up_weight, place, 0, keepdims=False)

    def up_half(which):
        return (
            lax.dynamic_slice_in_dim(up_one, which * half_q, half_q, 1),
            lax.dynamic_slice_in_dim(up_one, width_q + which * half_k, half_k, 1),
            lax.dynamic_slice_in_dim(up_one, width_q + width_k + which * half_k, half_k, 1),
        )

    up_other = swap_y(jnp.concatenate(up_half(1 - y), axis=1))
    share_down = lax.dynamic_index_in_dim(adapter_down_weight, place, 0, keepdims=False).T
    numbers = jnp.stack([row_adapter_index[:, 0], row_sequence_index])
    other_numbers = swap_y(numbers)
    down = [share_down, ring(share_down)]
    got_top, got_bottom, got_theirs, up_other, other_numbers, down = lax.optimization_barrier(
        (got_top, got_bottom, got_theirs, up_other, other_numbers, down)
    )
    share_q = jnp.where(x == 1, got_bottom, jnp.where(core == y, top, got_top))
    share_kv = jnp.where(x == 0, got_theirs, mine)
    up_own = jnp.concatenate(up_half(y), axis=1)
    up_pair = jnp.concatenate(
        [jnp.where(y == 0, up_own, up_other), jnp.where(y == 0, up_other, up_own)], axis=0
    )
    share_q = jnp.concatenate([share_q, up_pair[:, :half_q]], axis=0)
    share_kv = jnp.concatenate(
        [share_kv, up_pair[:, half_q : half_q + half_k], up_pair[:, half_q + half_k :]], axis=0
    )

    ids_own, ids_nb = numbers[0:1], other_numbers[0:1]
    seg_pair = jnp.where(
        y == 0,
        jnp.concatenate([numbers[1], other_numbers[1]]),
        jnp.concatenate([other_numbers[1], numbers[1]]),
    )
    normed_own = row_norm(residual_input, input_norm_gain)

    step, flip = np.arange(4).repeat(4), np.tile(np.arange(4), 4)
    chunk = (z + depth - step) % depth
    at_x = x + flip % 2 * (1 - 2 * x)
    at_core = core + flip // 2 * (1 - 2 * core)
    adapter = 2 * chunk * local + 2 * at_x + at_core
    scalars = jnp.stack(
        [
            (2 * chunk + at_core) * deep + at_x * (deep // 2),
            at_core,
            (2 * chunk + jnp.where(at_x == 1, y, 1 - y)) * deep,
            adapter,
            adapter + local,
            adapter + y * local,
        ]
    ).astype(jnp.int32)

    residual = jnp.split(residual_input, 4, axis=0)

    def group(ready, *values):
        return lax.optimization_barrier((values, ready))

    kv, q = [share_kv], [share_q]
    kv_x, kv_c, kv_xc, q_x, q_c, q_xc = [], [], [], [], [], []
    down_x, down_c, down_xc, other = [], [], [], []
    kv.append(ring(kv[0]))
    other.append(swap_y(residual[0]))
    kv_x.append(swap_x(kv[0]))
    kv_c.append(swap_core(kv[0]))
    down.append(ring(down[1]))
    down_x.append(swap_x(down[0]))
    down_c.append(swap_core(down[0]))
    for step in range(1, 4):
        (kv[step], kv_x[-1], part), _ = group((kv_c[-1],), kv[step], kv_x[-1], residual[step])
        if step < 3:
            kv.append(ring(kv[step]))
        other.append(swap_y(part))
        kv_x.append(swap_x(kv[step]))
        kv_c.append(swap_core(kv[step]))
        kv_xc.append(swap_core(kv_x[-2]))
        (onward_z, down[step], down_x[-1]), (_, other[-2]) = group(
            (down_c[-1], other[-2]),
            down[2] if step == 1 else q[-1],
            down[step],
            down_x[-1],
        )
        if step == 1:
            down[2] = onward_z
            down.append(ring(down[2]))
        else:
            q[-1] = onward_z
            q.append(ring(q[-1]))
        down_x.append(swap_x(down[step]))
        down_c.append(swap_core(down[step]))
        down_xc.append(swap_core(down_x[-2]))
    (q[0], kv_x[-1]), _ = group((kv_c[-1],), q[0], kv_x[-1])
    kv_xc.append(swap_core(kv_x[-1]))
    (down_x[-1],), (_, other[-1]) = group((down_c[-1], other[-1]), down_x[-1])
    down_xc.append(swap_core(down_x[-1]))
    def flat(*lists):
        return [piece for step in zip(*lists, strict=True) for piece in step]

    down_pieces = flat(down, down_x, down_c, down_xc)
    kv_pieces = flat(kv, kv_x, kv_c, kv_xc)
    normed_nb = row_norm(jnp.concatenate(other, axis=0), input_norm_gain)

    def tied(values, *ready):
        return lax.optimization_barrier((values, ready))[0]

    down_parts = Pieces(down_pieces, [(i, 0) for i in range(16)], down_pieces[0].shape[0])
    part_own, down_all = first_ranks(scalars, ids_own, normed_own, down_parts)
    q[2], part_own = tied((q[2], part_own))
    q.append(ring(q[2]))
    ranks_here = more_ranks(scalars, ids_nb, normed_nb, down_all, part_own, 16)
    ranks = (ranks_here, swap_y(ranks_here))
    gains = query_key_gains
    kv_all = Pieces(kv_pieces, [(i, 0) for i in range(16)], kv_pieces[0].shape[0])
    kv_heads = [
        keys_values(head, scalars, ids_own, ids_nb, gains, ranks, normed_own, normed_nb, kv_all)
        for head in range(half_k // HEAD_DIM)
    ]
    seg_before = halo(seg_pair)
    q_x = [swap_x(part) for part in q[:3]]
    kv_heads[0], seg_before, q, q_x[:2] = tied((kv_heads[0], seg_before, q, q_x[:2]))
    arriving = [halo(kv_heads[0]), halo(kv_heads[1])]
    q_x.append(swap_x(q[3]))
    q, q_x[:3] = tied((q, q_x[:3]), kv_heads[1])
    q_c = [swap_core(part) for part in q]
    q_xc = [swap_core(part) for part in q_x[:3]]
    q_x[3], arriving[0], q_c, q_xc = tied((q_x[3], arriving[0], q_c, q_xc))
    q_xc.append(swap_core(q_x[3]))
    q_pieces = flat(q, q_x, q_c, q_xc)
    project_queries = lambda head, ranks: queries_of(
        head, scalars, ids_own, ids_nb, gains, ranks, normed_own, normed_nb, q_pieces
    )
    seg_before = jnp.where((place == 0) & (z == 0), -1, seg_before)
    seg_span = jnp.concatenate([seg_before, seg_pair])

    spans = {}
    for name, parity in (("own", y), ("nb", 1 - y)):
        seg_keys = lax.dynamic_slice_in_dim(seg_span, parity * rows, 3 * rows, 0)[None, :]
        seg_rows = lax.dynamic_slice_in_dim(seg_pair, parity * rows, rows, 0)[:, None]
        places = jnp.stack([y, 1 - y, 2 + y, 3 - y]) - parity
        spans[name] = (places.astype(jnp.int32), seg_rows, seg_keys)
    where = jnp.stack([y, place, x, core]).astype(jnp.int32)
    kept, got, queries, last = [], [], [], ranks
    for head, both in enumerate(kv_heads):
        queries.append(project_queries(head, last))
        places, seg_rows, seg_keys = spans["nb"]
        sent = attend(1, places, queries[head], seg_rows, seg_keys, (arriving[head], both))
        got.append(swap_y(sent))
        last = tied(ranks, sent)
    for head, both in enumerate(kv_heads):
        places, seg_rows, seg_keys = spans["own"]
        mine = tied(queries[head], last)
        kept.append(attend(0, places, mine, seg_rows, seg_keys, (arriving[head], both)))
    return side_by_side(where, kept, got)


def paired(mesh, shapes):
    residual, _, weight, _, down = shapes[:5]
    rows = residual[0] // mesh.size
    return (
        mesh.shape["dp"] == 4
        and mesh.shape["adapter"] == 8
        and down[0] // mesh.shape["adapter"] == 4
        and rows % HEAD_DIM == 0
        and 2 * rows == WINDOW
        and weight[1] == (HEADS + 2 * KV_HEADS) * HEAD_DIM
        and weight[0] // mesh.shape["adapter"] % 32 == 0
    )


def solution(mesh):
    placed = (
        P(("dp", "adapter"), None),
        P(),
        P("adapter", "dp"),
        P(),
        P("adapter", None, None),
        P("adapter", None, None),
        P(("dp", "adapter"), None),
        P(("dp", "adapter")),
    )

    def whole(*arrays):
        body = paired_body if paired(mesh, [a.shape for a in arrays]) else general_body
        return jax.shard_map(
            body, mesh=mesh, in_specs=placed, out_specs=P(("dp", "adapter"), None), check_vma=False
        )(*arrays)

    return whole
```

```python
import functools
import math

import jax
import jax.numpy as jnp
import numpy as np
from jax import lax
from jax.experimental import pallas as pl
from jax.experimental.pallas import tpu as pltpu
from jax.sharding import PartitionSpec as P

HEADS = 8
KV_HEADS = 4
HEAD_DIM = 256
WINDOW = 1024


def shifted(value, axis, by):
    size = lax.axis_size(axis)
    pairs = [(i, i + by) for i in range(size) if 0 <= i + by < size]
    return lax.ppermute(value, axis, pairs)


def head_norm(block, heads, gain):
    shaped = block.reshape(block.shape[0], heads, HEAD_DIM)
    scaled = shaped * lax.rsqrt(jnp.mean(shaped * shaped, axis=-1, keepdims=True) + 1e-06) * gain
    return scaled.astype(jnp.bfloat16)


def adapter_delta(rank_values, up_matrices):
    width_q = HEADS * HEAD_DIM
    width_k = KV_HEADS * HEAD_DIM
    inner = up_matrices.shape[1]
    part_q = jnp.einsum(
        "nacr,arq->nacq",
        rank_values[..., 0:inner],
        up_matrices[:, :, 0:width_q],
        preferred_element_type=jnp.float32,
    )
    part_k = jnp.einsum(
        "nacr,arq->nacq",
        rank_values[..., inner : 2 * inner],
        up_matrices[:, :, width_q : width_q + width_k],
        preferred_element_type=jnp.float32,
    )
    part_v = jnp.einsum(
        "nacr,arq->nacq",
        rank_values[..., 2 * inner : 3 * inner],
        up_matrices[:, :, width_q + width_k :],
        preferred_element_type=jnp.float32,
    )
    return jnp.concatenate([part_q, part_k, part_v], axis=-1).astype(jnp.bfloat16)


def adapter_ranks(adapter_slots, down_matrices):
    return jnp.einsum(
        "nacd,adr->nacr", adapter_slots, down_matrices, preferred_element_type=jnp.float32
    ).astype(jnp.bfloat16)


def general_body(
    residual_input,
    input_norm_gain,
    base_projection_weight,
    query_key_gains,
    adapter_down_weight,
    adapter_up_weight,
    row_adapter_index,
    row_sequence_index,
):
    rows = residual_input.shape[0]
    width = residual_input.shape[1]
    width_q = HEADS * HEAD_DIM
    width_k = KV_HEADS * HEAD_DIM
    group = HEADS // KV_HEADS
    values_in = residual_input.astype(jnp.float32)
    normed = (
        values_in
        * lax.rsqrt(jnp.mean(values_in * values_in, axis=-1, keepdims=True) + 1e-06)
        * input_norm_gain
    ).astype(jnp.bfloat16)
    slab = lax.all_gather(base_projection_weight, "dp", axis=1, tiled=True)
    base = jnp.dot(
        normed,
        lax.all_gather(slab, "adapter", axis=0, tiled=True),
        preferred_element_type=jnp.float32,
    ).astype(jnp.bfloat16)
    total_width = base.shape[1]
    owners = lax.axis_size("adapter")
    local_adapter_count = adapter_down_weight.shape[0]
    adapters_all = owners * local_adapter_count
    capacity = 2 * rows // adapters_all
    adapter_ids = row_adapter_index[:, 0]
    onehot = (adapter_ids[:, None] == jnp.arange(adapters_all, dtype=jnp.int32)[None, :]).astype(
        jnp.int32
    )
    earlier = jnp.cumsum(onehot, axis=0) - onehot
    place = jnp.sum(earlier * onehot, axis=1)
    slot = adapter_ids * capacity + place
    scratch_buffer = jnp.zeros((adapters_all * capacity, width), jnp.bfloat16).at[slot].set(normed)
    scratch_buffer = scratch_buffer.reshape(owners, local_adapter_count, capacity, width)
    adapter_corrections = adapter_delta(
        adapter_ranks(
            lax.all_to_all(scratch_buffer, "adapter", split_axis=0, concat_axis=0, tiled=True),
            adapter_down_weight,
        ),
        adapter_up_weight,
    )
    returned = lax.all_to_all(
        adapter_corrections, "adapter", split_axis=0, concat_axis=0, tiled=True
    )
    delta_slots = returned.reshape(adapters_all * capacity, total_width)
    delta_update = delta_slots[slot]
    projected = base.astype(jnp.float32) + delta_update.astype(jnp.float32)
    queries = head_norm(projected[:, 0:width_q], HEADS, query_key_gains[0]).reshape(
        rows, KV_HEADS, group, HEAD_DIM
    )
    keys = head_norm(
        projected[:, width_q : width_q + width_k], KV_HEADS, query_key_gains[1]
    ).reshape(rows, width_k)
    values = projected[:, width_q + width_k :].astype(jnp.bfloat16)
    before = (WINDOW + rows - 2) // rows
    key_parts = []
    value_parts = []
    seg_parts = []
    for offset in range(before, 0, -1):
        moved_keys, moved_values, moved_seg = shifted(
            (keys, values, row_sequence_index), ("dp", "adapter"), offset
        )
        key_parts.append(moved_keys)
        value_parts.append(moved_values)
        seg_parts.append(moved_seg)
    key_parts.append(keys)
    value_parts.append(values)
    seg_parts.append(row_sequence_index)
    span = (before + 1) * rows
    key_all = jnp.concatenate(key_parts, axis=0).reshape(span, KV_HEADS, HEAD_DIM)
    value_all = jnp.concatenate(value_parts, axis=0).reshape(span, KV_HEADS, HEAD_DIM)
    seg_all = jnp.concatenate(seg_parts, axis=0)
    position = lax.axis_index(("dp", "adapter"))
    query_pos = position * rows + jnp.arange(rows, dtype=jnp.int32)
    key_pos = (position - before) * rows + jnp.arange(span, dtype=jnp.int32)
    gap = query_pos[:, None] - key_pos[None, :]
    allowed = (
        (row_sequence_index[:, None] == seg_all[None, :])
        & (gap >= 0)
        & (gap < WINDOW)
        & (key_pos[None, :] >= 0)
    )
    scores = jnp.einsum(
        "tkgd,skd->kgts", queries, key_all, preferred_element_type=jnp.float32
    ) * HEAD_DIM ** (-0.5)
    weights = jnp.where(allowed[None, None], jnp.exp(scores), jnp.float32(0.0))
    total = jnp.sum(weights, axis=-1)
    probs = weights.astype(jnp.bfloat16)
    summed = jnp.einsum("kgts,skd->tkgd", probs, value_all, preferred_element_type=jnp.float32)
    result = summed / jnp.transpose(total, (2, 0, 1))[..., None]
    return result.reshape(rows, width_q).astype(jnp.bfloat16)


BF16 = jnp.bfloat16
F32 = jnp.float32
ANY = pl.BlockSpec(memory_space=pl.ANY)
SMEM = pl.BlockSpec(memory_space=pltpu.SMEM)
VMEM = pl.BlockSpec(memory_space=pltpu.VMEM)
SMALL = pl.CostEstimate(flops=1, bytes_accessed=1, transcendentals=0)
Q_ROW, KV_KIND, KV_ROW, UP_EVEN, UP_ODD, DOWN_ID = range(6)


def params(mib):
    return pltpu.CompilerParams(vmem_limit_bytes=mib << 20)


def route(value, depth, rule):
    pairs = []
    for x in range(2):
        for core in range(2):
            for z in range(depth):
                for y in range(2):
                    to = rule(x, core, z, y)
                    if to is not None:
                        source = (2 * x + core) * 2 * depth + 2 * z + y
                        pairs.append((source, (2 * to[0] + to[1]) * 2 * depth + 2 * to[2] + to[3]))
    return lax.ppermute(value, ("dp", "adapter"), pairs)


def after(value, *others):
    return lax.optimization_barrier((value, others))[0]


def row_norm(values, gain):
    values = values.astype(F32)
    scale = lax.rsqrt(jnp.mean(values * values, axis=-1, keepdims=True) + 1e-06)
    return (values * scale * gain).astype(BF16)


def copies_done(copies):
    for copy in copies:
        copy.start()
    for copy in copies:
        copy.wait()


def masked_ranks(scalars, ids, down, normed, out, count, waits=((),)):
    deep, share = out.shape[0], count // len(waits)
    total = jnp.zeros(out.shape, F32)
    for part, copies in enumerate(waits):
        for copy in copies:
            copy.wait()
        every = lax.dot_general(
            down[part * share * deep : (part + 1) * share * deep],
            normed[...],
            (((1,), (1,)), ((), ())),
            preferred_element_type=F32,
        )
        for i in range(share):
            mine = ids[...] == scalars[DOWN_ID, part * share + i]
            total = total + jnp.where(mine, every[i * deep : (i + 1) * deep], 0.0)
    out[...] = total.astype(BF16)


def rank_kernel(count, scalars, ids, normed, down, first, out):
    out[0] = first[...]
    masked_ranks(scalars, ids, down, normed, out.at[1], count)


def first_rank_kernel(pieces, scalars, ids, normed, *refs):
    held = refs[: len(pieces.arrays)]
    out, down, sems = refs[len(pieces.arrays) :]
    deep, count = pieces.deep, len(pieces.names)
    copies = [
        pltpu.make_async_copy(
            pieces.cut(held, i, 0, deep), down.at[pl.ds(i * deep, deep)], sems.at[i]
        )
        for i in range(count)
    ]
    for copy in copies:
        copy.start()
    masked_ranks(scalars, ids, down, normed, out, count, (copies[: count // 2], copies[count // 2 :]))


def first_ranks(scalars, ids, normed, pieces):
    rows, width = normed.shape
    count, deep = len(pieces.names), pieces.deep
    return pl.pallas_call(
        functools.partial(first_rank_kernel, pieces),
        out_shape=[
            jax.ShapeDtypeStruct((deep, rows), BF16),
            jax.ShapeDtypeStruct((count * deep, width), BF16),
        ],
        in_specs=[SMEM, VMEM, VMEM] + [ANY] * len(pieces.arrays),
        out_specs=[VMEM, VMEM],
        scratch_shapes=[pltpu.SemaphoreType.DMA((count,))],
        compiler_params=params(24),
        cost_estimate=SMALL,
    )(scalars, ids, normed, *pieces.arrays)


def more_ranks(scalars, ids, normed, down, first, count):
    rows, width = normed.shape
    return pl.pallas_call(
        functools.partial(rank_kernel, count),
        out_shape=jax.ShapeDtypeStruct((2, down.shape[0] // count, rows), BF16),
        in_specs=[SMEM, VMEM, VMEM, VMEM, VMEM],
        out_specs=VMEM,
        compiler_params=params(24),
        cost_estimate=SMALL,
    )(scalars, ids, normed, down, first)


def spread(ranks, ids, scalars, count, into):
    inner = ranks.shape[0]
    for i in range(count):
        for odd in range(2):
            mine = ids[...] == scalars[UP_EVEN + odd, i]
            at = (2 * i + odd) * inner
            into[at : at + inner, :] = jnp.where(mine, ranks, jnp.zeros_like(ranks))


def project(normed, weight, into, up):
    base = jnp.dot(normed, weight, preferred_element_type=F32).astype(BF16)
    delta = lax.dot_general(
        into, up, (((0,), (0,)), ((), ())), preferred_element_type=F32
    ).astype(BF16)
    return base.astype(F32) + delta.astype(F32)


def unit(block, gain):
    scale = lax.rsqrt(jnp.mean(block * block, axis=-1, keepdims=True) + 1e-06)
    return (block * scale * gain).astype(BF16)


class Pieces:
    def __init__(self, arrays, names, deep):
        self.arrays, self.names, self.deep = arrays, names, deep

    def cut(self, refs, i, start, size, columns=None):
        array, at = self.names[i]
        rows = pl.ds(at * self.deep + start, size)
        return refs[array].at[rows] if columns is None else refs[array].at[rows, columns]


def kv_kernel(pieces, inner, head, *refs):
    scalars, ids_own, ids_nb, gains = refs[:4]
    ranks, ranks_there = refs[4:6]
    normed = refs[6:8]
    held = refs[8 : 8 + len(pieces.arrays)]
    out, weight, up, into, sems = refs[8 + len(pieces.arrays) :]
    deep, count = pieces.deep - 4 * inner, len(pieces.names)
    columns = pl.ds(head * HEAD_DIM, HEAD_DIM)
    copies = []
    for i in range(count):
        kind = scalars[KV_KIND, i]
        row = pl.multiple_of(scalars[KV_ROW, i], deep)
        copies.append(
            pltpu.make_async_copy(
                pieces.cut(held, i, 0, deep, columns),
                weight.at[kind, pl.ds(row, deep)],
                sems.at[3 * i],
            )
        )
        for both in range(2):
            copies.append(
                pltpu.make_async_copy(
                    pieces.cut(held, i, deep + 2 * inner * both, 2 * inner, columns),
                    up.at[both, pl.ds(2 * inner * i, 2 * inner)],
                    sems.at[3 * i + 1 + both],
                )
            )
    for copy in copies:
        copy.start()
    for side, ids in ((0, ids_own), (1, ids_nb)):
        both = ranks[side] + ranks_there[1 - side]
        for kind in range(2):
            part = both[(1 + kind) * inner : (2 + kind) * inner]
            spread(part, ids, scalars, count, into.at[2 * side + kind])
    for copy in copies:
        copy.wait()
    for side in range(2):
        keys = project(normed[side][...], weight[0], into[2 * side], up[0])
        out[side, :, 0:HEAD_DIM] = unit(keys, gains[1:2, :])
        values = project(normed[side][...], weight[1], into[2 * side + 1], up[1])
        out[side, :, HEAD_DIM:] = values.astype(BF16)


def keys_values(head, scalars, ids_own, ids_nb, gains, ranks, normed_own, normed_nb, pieces):
    rows, width = normed_own.shape
    count, inner = len(pieces.names), ranks[0].shape[1] // 3
    return pl.pallas_call(
        functools.partial(kv_kernel, pieces, inner, head),
        out_shape=jax.ShapeDtypeStruct((2, rows, 2 * HEAD_DIM), BF16),
        in_specs=[SMEM] + [VMEM] * 7 + [ANY] * len(pieces.arrays),
        out_specs=VMEM,
        scratch_shapes=[
            pltpu.VMEM((2, width, HEAD_DIM), BF16),
            pltpu.VMEM((2, 2 * inner * count, HEAD_DIM), BF16),
            pltpu.VMEM((4, 2 * inner * count, rows), BF16),
            pltpu.SemaphoreType.DMA((3 * count,)),
        ],
        compiler_params=params(32),
        cost_estimate=SMALL,
    )(scalars, ids_own, ids_nb, gains, *ranks, normed_own, normed_nb, *pieces.arrays)


def query_kernel(count, inner, start, sides, *refs):
    scalars, gains, ranks, ranks_there = refs[:4]
    ids, rows_in = refs[4 : 4 + len(sides)], refs[4 + len(sides) : 4 + 2 * len(sides)]
    pieces = refs[4 + 2 * len(sides) : 4 + 2 * len(sides) + count]
    out, weight, up, into, normed, sems = refs[4 + 2 * len(sides) + count :]
    deep = pieces[0].shape[0] - 2 * inner
    columns = pl.ds(start, weight.shape[1])
    whole = [
        pltpu.make_async_copy(rows_in[i], normed.at[i], sems.at[2 * count + i])
        for i in range(len(sides))
    ]
    whole[0].start()
    copies = []
    for i in range(count):
        row = pl.multiple_of(scalars[Q_ROW, i], deep)
        copies.append(
            pltpu.make_async_copy(
                pieces[i].at[pl.ds(0, deep), columns],
                weight.at[pl.ds(row, deep)],
                sems.at[2 * i],
            )
        )
        copies.append(
            pltpu.make_async_copy(
                pieces[i].at[pl.ds(deep, 2 * inner), columns],
                up.at[pl.ds(2 * inner * i, 2 * inner)],
                sems.at[2 * i + 1],
            )
        )
    for copy in copies + whole[1:]:
        copy.start()
    for i, side in enumerate(sides):
        both = ranks[side, 0:inner] + ranks_there[1 - side, 0:inner]
        spread(both, ids[i], scalars, count, into.at[i])
    for copy in copies:
        copy.wait()
    for i in range(len(sides)):
        whole[i].wait()
        for at in range(weight.shape[1] // HEAD_DIM):
            cut = slice(at * HEAD_DIM, (at + 1) * HEAD_DIM)
            block = project(normed[i], weight[:, cut], into[i], up[:, cut])
            out[i, :, cut] = unit(block, gains[0:1, :])


def queries_of(start, columns, sides, scalars, ids, gains, ranks, normed, pieces):
    rows, width = normed[0].shape
    count, inner, several = len(pieces), ranks[0].shape[1] // 3, len(sides)
    chosen = [ids[side] for side in sides] + [normed[side] for side in sides]
    return pl.pallas_call(
        functools.partial(query_kernel, count, inner, start, sides),
        out_shape=jax.ShapeDtypeStruct((several, rows, columns), BF16),
        in_specs=[SMEM] + [VMEM] * (3 + several) + [ANY] * (several + count),
        out_specs=VMEM,
        scratch_shapes=[
            pltpu.VMEM((width, columns), BF16),
            pltpu.VMEM((2 * inner * count, columns), BF16),
            pltpu.VMEM((several, 2 * inner * count, rows), BF16),
            pltpu.VMEM((several, rows, width), BF16),
            pltpu.SemaphoreType.DMA((2 * count + several,)),
        ],
        compiler_params=params(56),
        cost_estimate=SMALL,
    )(scalars, gains, *ranks, *chosen, *pieces)


def attend_kernel(places, queries, seg_rows, seg_keys, *refs):
    before, here_too, out, held, sems = refs
    blocks = [before.at[0], before.at[1], here_too.at[0], here_too.at[1]]
    rows = queries.shape[0]
    slots = held.shape[0]
    for wait in (False, True):
        for i in range(4):
            slot = places[i]

            @pl.when((slot >= 0) & (slot < slots))
            def _():
                copy = pltpu.make_async_copy(blocks[i], held.at[slot], sems.at[i])
                if wait:
                    copy.wait()
                else:
                    copy.start()

    tile = HEAD_DIM
    heads = queries.shape[1] // HEAD_DIM
    tiles = WINDOW // tile + 1
    per_block = rows // tile
    row = lax.broadcasted_iota(jnp.int32, (tile, tile), 0)
    column = lax.broadcasted_iota(jnp.int32, (tile, tile), 1)
    for part in range(rows // tile):
        here = slice(part * tile, (part + 1) * tile)
        query = jnp.concatenate(
            [queries[here, h * HEAD_DIM : (h + 1) * HEAD_DIM] for h in range(heads)], axis=0
        )
        total = jnp.zeros((heads * tile, 128), F32)
        summed = jnp.zeros((heads * tile, HEAD_DIM), F32)
        for step in range(tiles):
            at = part + step
            block, inside = at // per_block, at % per_block
            span = slice(inside * tile, (inside + 1) * tile)
            keys = held[block, span, 0:HEAD_DIM]
            values = held[block, span, HEAD_DIM:]
            allowed = seg_rows[here, :] == seg_keys[:, at * tile : (at + 1) * tile]
            if step == 0:
                allowed = allowed & (column > row)
            if step == tiles - 1:
                allowed = allowed & (column <= row)
            scores = lax.dot_general(
                query, keys, (((1,), (1,)), ((), ())), preferred_element_type=F32
            )
            weights = jnp.exp2(scores * (HEAD_DIM ** (-0.5) * math.log2(math.e)))
            weights = jnp.where(jnp.concatenate([allowed] * heads, axis=0), weights, 0.0)
            for cut in range(tile // 128):
                total = total + weights[:, cut * 128 : (cut + 1) * 128]
            summed = summed + jnp.dot(
                weights.astype(BF16), values, preferred_element_type=F32
            )
        result = summed / jnp.sum(total, axis=-1, keepdims=True)
        for h in range(heads):
            out[here, h * HEAD_DIM : (h + 1) * HEAD_DIM] = result[
                h * tile : (h + 1) * tile
            ].astype(BF16)


def attend(at, places, queries, seg_rows, seg_keys, blocks):
    rows, width = queries.shape[1:]
    slots = seg_keys.shape[1] // rows
    return pl.pallas_call(
        attend_kernel,
        grid=(1,),
        out_shape=jax.ShapeDtypeStruct((rows, width), BF16),
        in_specs=[
            SMEM,
            pl.BlockSpec((None, rows, width), lambda i: (at, 0, 0)),
            pl.BlockSpec((rows, 1), lambda i: (0, 0)),
            pl.BlockSpec((1, slots * rows), lambda i: (0, 0)),
        ]
        + [ANY] * 2,
        out_specs=pl.BlockSpec((rows, width), lambda i: (0, 0)),
        scratch_shapes=[
            pltpu.VMEM((slots, rows, 2 * HEAD_DIM), BF16),
            pltpu.SemaphoreType.DMA((4,)),
        ],
        compiler_params=params(24),
        cost_estimate=SMALL,
    )(places, queries, seg_rows, seg_keys, *blocks)


def side_kernel(count, where, *refs):
    y = where[0]
    out = refs[2 * count]
    width = refs[0].shape[1]
    for side, at in ((0, y), (1, 1 - y)):
        for i in range(count):
            start = pl.multiple_of((at * count + i) * width, width)
            out[:, pl.ds(start, width)] = refs[side * count + i][...]


def side_by_side(where, kept, got):
    rows, width = kept[0].shape
    return pl.pallas_call(
        functools.partial(side_kernel, len(kept)),
        out_shape=jax.ShapeDtypeStruct((rows, 2 * width * len(kept)), BF16),
        in_specs=[SMEM] + [VMEM] * (2 * len(kept)),
        out_specs=VMEM,
        compiler_params=params(16),
        cost_estimate=SMALL,
    )(where, *kept, *got)


def paired_body(
    residual_input,
    input_norm_gain,
    base_projection_weight,
    query_key_gains,
    adapter_down_weight,
    adapter_up_weight,
    row_adapter_index,
    row_sequence_index,
):
    rows = residual_input.shape[0]
    width_q, width_k = HEADS * HEAD_DIM, KV_HEADS * HEAD_DIM
    half_q, half_k = width_q // 2, width_k // 2
    depth = lax.axis_size("adapter") // 2
    local = adapter_down_weight.shape[0]
    deep = base_projection_weight.shape[0]
    place = lax.axis_index("dp")
    x, core = place // 2, place % 2
    owner = lax.axis_index("adapter")
    z, y = owner // 2, owner % 2
    swap_y = lambda v: route(v, depth, lambda x, c, z, y: (x, c, z, 1 - y))
    swap_x = lambda v: route(v, depth, lambda x, c, z, y: (1 - x, c, z, y))
    swap_core = lambda v: route(v, depth, lambda x, c, z, y: (x, 1 - c, z, y))
    ring = lambda v: route(v, depth, lambda x, c, z, y: (x, c, (z + 1) % depth, y))

    def onward(x, c, z, y):
        if z + 1 < depth:
            return (x, c, z + 1, y)
        after = 2 * x + c + 1
        return (after // 2, after % 2, 0, y) if after < 4 else None

    halo = lambda v: route(v, depth, onward)

    block = base_projection_weight
    top, bottom = block[: deep // 2], block[deep // 2 :]
    mine = lax.dynamic_slice_in_dim(block, y * half_k, half_k, 1)
    theirs = lax.dynamic_slice_in_dim(block, (1 - y) * half_k, half_k, 1)
    got_top = route(top, depth, lambda x, c, z, y: (0, y, z, c) if x == 0 and c != y else None)
    got_bottom = route(bottom, depth, lambda x, c, z, y: (1, y, z, c) if x == 0 else None)
    got_theirs = route(
        theirs, depth, lambda x, c, z, y: (0, c, z, 1 - y) if x == 1 else None
    )
    up_one = lax.dynamic_index_in_dim(adapter_up_weight, place, 0, keepdims=False)

    def up_half(which):
        return (
            lax.dynamic_slice_in_dim(up_one, which * half_q, half_q, 1),
            lax.dynamic_slice_in_dim(up_one, width_q + which * half_k, half_k, 1),
            lax.dynamic_slice_in_dim(up_one, width_q + width_k + which * half_k, half_k, 1),
        )

    up_other = swap_y(jnp.concatenate(up_half(1 - y), axis=1))
    share_down = lax.dynamic_index_in_dim(adapter_down_weight, place, 0, keepdims=False).T
    numbers = jnp.stack([row_adapter_index[:, 0], row_sequence_index])
    other_numbers = swap_y(numbers)
    down = [share_down, ring(share_down)]
    got_top, got_bottom, got_theirs, up_other, other_numbers, down = lax.optimization_barrier(
        (got_top, got_bottom, got_theirs, up_other, other_numbers, down)
    )
    share_q = jnp.where(x == 1, got_bottom, jnp.where(core == y, top, got_top))
    share_kv = jnp.where(x == 0, got_theirs, mine)
    up_own = jnp.concatenate(up_half(y), axis=1)
    up_pair = jnp.concatenate(
        [jnp.where(y == 0, up_own, up_other), jnp.where(y == 0, up_other, up_own)], axis=0
    )
    share_q = jnp.concatenate([share_q, up_pair[:, :half_q]], axis=0)
    share_kv = jnp.concatenate(
        [share_kv, up_pair[:, half_q : half_q + half_k], up_pair[:, half_q + half_k :]], axis=0
    )

    ids_own, ids_nb = numbers[0:1], other_numbers[0:1]
    seg_pair = jnp.where(
        y == 0,
        jnp.concatenate([numbers[1], other_numbers[1]]),
        jnp.concatenate([other_numbers[1], numbers[1]]),
    )
    normed_own = row_norm(residual_input, input_norm_gain)

    step, flip = np.arange(4).repeat(4), np.tile(np.arange(4), 4)
    chunk = (z + depth - step) % depth
    at_x = x + flip % 2 * (1 - 2 * x)
    at_core = core + flip // 2 * (1 - 2 * core)
    adapter = 2 * chunk * local + 2 * at_x + at_core
    scalars = jnp.stack(
        [
            (2 * chunk + at_core) * deep + at_x * (deep // 2),
            at_core,
            (2 * chunk + jnp.where(at_x == 1, y, 1 - y)) * deep,
            adapter,
            adapter + local,
            adapter + y * local,
        ]
    ).astype(jnp.int32)

    residual = jnp.split(residual_input, 4, axis=0)

    def group(ready, *values):
        return lax.optimization_barrier((values, ready))

    kv, q = [share_kv], [share_q]
    kv_x, kv_c, kv_xc, q_x, q_c, q_xc = [], [], [], [], [], []
    down_x, down_c, down_xc, other = [], [], [], []
    kv.append(ring(kv[0]))
    other.append(swap_y(residual[0]))
    kv_x.append(swap_x(kv[0]))
    kv_c.append(swap_core(kv[0]))
    down.append(ring(down[1]))
    down_x.append(swap_x(down[0]))
    down_c.append(swap_core(down[0]))
    for step in range(1, 4):
        (kv[step], kv_x[-1], part), _ = group((kv_c[-1],), kv[step], kv_x[-1], residual[step])
        if step < 3:
            kv.append(ring(kv[step]))
        other.append(swap_y(part))
        kv_x.append(swap_x(kv[step]))
        kv_c.append(swap_core(kv[step]))
        kv_xc.append(swap_core(kv_x[-2]))
        (onward_z, down[step], down_x[-1]), (_, other[-2]) = group(
            (down_c[-1], other[-2]),
            down[2] if step == 1 else q[-1],
            down[step],
            down_x[-1],
        )
        if step == 1:
            down[2] = onward_z
            down.append(ring(down[2]))
        else:
            q[-1] = onward_z
            q.append(ring(q[-1]))
        down_x.append(swap_x(down[step]))
        down_c.append(swap_core(down[step]))
        down_xc.append(swap_core(down_x[-2]))
    (q[0], kv_x[-1]), _ = group((kv_c[-1],), q[0], kv_x[-1])
    kv_xc.append(swap_core(kv_x[-1]))
    (down_x[-1],), (_, other[-1]) = group((down_c[-1], other[-1]), down_x[-1])
    down_xc.append(swap_core(down_x[-1]))
    def flat(*lists):
        return [piece for step in zip(*lists, strict=True) for piece in step]

    down_pieces = flat(down, down_x, down_c, down_xc)
    kv_pieces = flat(kv, kv_x, kv_c, kv_xc)
    normed_nb = row_norm(jnp.concatenate(other, axis=0), input_norm_gain)

    def tied(values, *ready):
        return lax.optimization_barrier((values, ready))[0]

    down_parts = Pieces(down_pieces, [(i, 0) for i in range(16)], down_pieces[0].shape[0])
    part_own, down_all = first_ranks(scalars, ids_own, normed_own, down_parts)
    q[2], part_own = tied((q[2], part_own))
    q.append(ring(q[2]))
    ranks_here = more_ranks(scalars, ids_nb, normed_nb, down_all, part_own, 16)
    ranks = (ranks_here, swap_y(ranks_here))
    gains = query_key_gains
    kv_all = Pieces(kv_pieces, [(i, 0) for i in range(16)], kv_pieces[0].shape[0])
    kv_heads = [
        keys_values(head, scalars, ids_own, ids_nb, gains, ranks, normed_own, normed_nb, kv_all)
        for head in range(half_k // HEAD_DIM)
    ]
    seg_before = halo(seg_pair)
    q_x = [swap_x(part) for part in q[:3]]
    kv_heads[0], seg_before, q, q_x[:2] = tied((kv_heads[0], seg_before, q, q_x[:2]))
    arriving = [halo(kv_heads[0]), halo(kv_heads[1])]
    q_x.append(swap_x(q[3]))
    q, q_x[:3] = tied((q, q_x[:3]), kv_heads[1])
    q_c = [swap_core(part) for part in q]
    q_xc = [swap_core(part) for part in q_x[:3]]
    q_x[3], arriving[0], q_c, q_xc = tied((q_x[3], arriving[0], q_c, q_xc))
    q_xc.append(swap_core(q_x[3]))
    q_pieces = flat(q, q_x, q_c, q_xc)
    def project_queries(head, sides, ranks):
        width = half_q // len(kv_heads)
        both_ids, both_rows = (ids_own, ids_nb), (normed_own, normed_nb)
        return queries_of(
            head * width, width, sides, scalars, both_ids, gains, ranks, both_rows, q_pieces
        )

    seg_before = jnp.where((place == 0) & (z == 0), -1, seg_before)
    seg_span = jnp.concatenate([seg_before, seg_pair])

    spans = {}
    for name, parity in (("own", y), ("nb", 1 - y)):
        seg_keys = lax.dynamic_slice_in_dim(seg_span, parity * rows, 3 * rows, 0)[None, :]
        seg_rows = lax.dynamic_slice_in_dim(seg_pair, parity * rows, rows, 0)[:, None]
        places = jnp.stack([y, 1 - y, 2 + y, 3 - y]) - parity
        spans[name] = (places.astype(jnp.int32), seg_rows, seg_keys)
    where = jnp.stack([y, place, x, core]).astype(jnp.int32)
    queries, got, last = [], [], ranks
    for head, both in enumerate(kv_heads):
        queries.append(project_queries(head, (0, 1) if head else (1,), last))
        at = queries[head].shape[0] - 1
        sent = attend(at, spans["nb"][0], queries[head], *spans["nb"][1:], (arriving[head], both))
        got.append(swap_y(sent))
        last = tied(ranks, sent)
    queries[0] = project_queries(0, (0,), last)
    kept = [
        attend(0, spans["own"][0], queries[head], *spans["own"][1:], (arriving[head], both))
        for head, both in enumerate(kv_heads)
    ]
    return side_by_side(where, kept, got)


def paired(mesh, shapes):
    residual, _, weight, _, down = shapes[:5]
    rows = residual[0] // mesh.size
    return (
        mesh.shape["dp"] == 4
        and mesh.shape["adapter"] == 8
        and down[0] // mesh.shape["adapter"] == 4
        and rows % HEAD_DIM == 0
        and 2 * rows == WINDOW
        and weight[1] == (HEADS + 2 * KV_HEADS) * HEAD_DIM
        and weight[0] // mesh.shape["adapter"] % 32 == 0
    )


def solution(mesh):
    placed = (
        P(("dp", "adapter"), None),
        P(),
        P("adapter", "dp"),
        P(),
        P("adapter", None, None),
        P("adapter", None, None),
        P(("dp", "adapter"), None),
        P(("dp", "adapter")),
    )

    def whole(*arrays):
        body = paired_body if paired(mesh, [a.shape for a in arrays]) else general_body
        return jax.shard_map(
            body, mesh=mesh, in_specs=placed, out_specs=P(("dp", "adapter"), None), check_vma=False
        )(*arrays)

    return whole
```
